256 devices in a mesh: wide: 64 (over x_hi, z, y), narrow: 4 (over x_lo, core).
Axes of the slice: x: 4 (x_hi: 2, x_lo: 2; x = x_hi * 2 + x_lo), y: 4, z: 8, core: 2. Of those that a mesh axis runs over, the one named last changes fastest.
Arguments:
- attention: bfloat16 [256, 16384], P(None, 'wide'), may hold values from -6 to 6
- out_proj: bfloat16 [16384, 8192], P('wide', 'narrow'), may hold values from -0.0625 to 0.0625
- residual: bfloat16 [512, 8192], P('wide', 'narrow'), may hold values from -6 to 6
- dictionary: bfloat16 [2, 8192, 32768], P(None, 'narrow', 'wide'), may hold values from -0.046875 to 0.046875
- enc_bias: float32 [32768], P('wide'), may hold values from -3 to 3
- active: int32 [256, 32768], P(None, 'wide'), may hold values 0 or 1
Outputs:
- grad_dictionary: bfloat16 [2, 8192, 32768], P(None, 'narrow', 'wide')
- grad_bias: float32 [32768], P('wide')
The draws below stay inside these ranges and needn't reach their ends.
All inputs are finite; a program needn't handle non-finite values. No bound on the sum of `active` on one device may be relied on, other than what follows from the above.
Results may differ from the reference program's by a relative error of at most 0.01.
Values may be sent and summed in bfloat16 or wider, within the bound.
A program may use at most 64 MiB of HBM per device.

```python
import jax
import jax.numpy as jnp
from jax import lax

D = 8192
LATENTS = 32768
TOKENS = 256


def place_ends(drawn, stream_key, low, high):
    shape = drawn.shape
    spot = [jax.random.randint(jax.random.fold_in(stream_key, axis), (), 0, shape[axis]) for axis in range(len(shape))]
    drawn = drawn.at[tuple(spot)].set(low)
    longest = shape.index(max(shape))
    spot[longest] = (spot[longest] + 1) % shape[longest]
    return drawn.at[tuple(spot)].set(high)


def levels(key, extent, shards, low, largest):
    def one(axis_at, blocks):
        draws = jax.random.uniform(jax.random.fold_in(jax.random.fold_in(key, 6), axis_at), (blocks,), jnp.float32, low / len(shards), largest / len(shards))
        return jnp.repeat(jnp.exp(draws), extent[axis_at] // blocks).reshape((-1,) + (1,) * (len(extent) - axis_at - 1))

    gain = one(*shards[0])
    for cut in shards[1:]:
        gain = gain * one(*cut)
    return gain


def bell_draw(rng, shape, scale, most, split=(), held_as=jnp.bfloat16):
    gain = levels(rng, shape, split, -0.22, 0.18) if split else 1.0
    array = jax.random.normal(rng, shape, jnp.float32) * scale * gain
    return jnp.minimum(jnp.maximum(array, -most), most).astype(held_as)


def setup_inputs(seed: int = 0) -> dict:
    arg_keys = jax.random.split(jax.random.key(seed), 7)
    return {
        "attention": bell_draw(arg_keys[0], (TOKENS, 2 * D), 1.0, 6.0, ((1, 64),)),
        "out_proj": bell_draw(arg_keys[1], (2 * D, D), D ** -0.5, 0.0625, ((0, 64), (1, 4))),
        "residual": bell_draw(arg_keys[2], (2 * TOKENS, D), 1.0, 6.0, ((0, 64), (1, 4))),
        "dictionary": bell_draw(arg_keys[3], (2, D, LATENTS), (2 * D) ** -0.5, 0.046875, ((1, 4), (2, 64))),
        "enc_bias": bell_draw(arg_keys[4], (LATENTS,), 0.5, 3.0, ((0, 64),), jnp.float32),
        "active": place_ends((jax.random.randint(arg_keys[5], (TOKENS, LATENTS), 0, 64) < 1).astype(jnp.int32), jax.random.fold_in(arg_keys[5], 1), 0, 1),
    }


def reference(attention, out_proj, residual, dictionary, enc_bias, active):
    highest = lax.Precision.HIGHEST
    blocks = []
    for member in range(2):
        attn_cols = attention[:, member * D:(member + 1) * D].astype(jnp.float32)
        proj_rows = out_proj[member * D:(member + 1) * D].astype(jnp.float32)
        resid_rows = residual[member * TOKENS:(member + 1) * TOKENS].astype(jnp.float32)
        summed = resid_rows + jnp.dot(attn_cols, proj_rows, precision=highest)
        blocks.append(summed.astype(jnp.bfloat16))
    stacked = jnp.concatenate(blocks, axis=1)
    stacked_f = stacked.astype(jnp.float32)
    flat_dict = dictionary.reshape(2 * D, LATENTS)
    block_width = min(LATENTS, 2048)
    block_count = LATENTS // block_width
    starts = jnp.arange(block_count, dtype=jnp.int32) * block_width

    def encode(carry, offset):
        cols = lax.dynamic_slice_in_dim(flat_dict, offset, block_width, 1).astype(jnp.float32)
        bias = lax.dynamic_slice_in_dim(enc_bias, offset, block_width, 0)
        mask = lax.dynamic_slice_in_dim(active, offset, block_width, 1).astype(jnp.float32)
        preact = jnp.dot(stacked_f, cols, precision=highest) + bias
        feat = (mask * preact).astype(jnp.bfloat16)
        carry = carry + lax.dot_general(feat.astype(jnp.float32), cols, (((1,), (1,)), ((), ())), precision=highest)
        return carry, feat

    recon, feat_blocks = lax.scan(encode, jnp.zeros((TOKENS, 2 * D), jnp.float32), starts)
    errors = (recon - stacked_f).astype(jnp.bfloat16)
    errors_f = errors.astype(jnp.float32)

    def backward(pair):
        offset, feat = pair
        cols = lax.dynamic_slice_in_dim(flat_dict, offset, block_width, 1).astype(jnp.float32)
        mask = lax.dynamic_slice_in_dim(active, offset, block_width, 1).astype(jnp.float32)
        grad_feat = jnp.dot(errors_f, cols, precision=highest)
        grad_pre = (mask * grad_feat).astype(jnp.bfloat16).astype(jnp.float32)
        bias_grad = jnp.sum(grad_pre, axis=0)
        total = lax.dot_general(stacked_f, grad_pre, (((0,), (0,)), ((), ())), precision=highest)
        total = total + lax.dot_general(errors_f, feat.astype(jnp.float32), (((0,), (0,)), ((), ())), precision=highest)
        return total.astype(jnp.bfloat16), bias_grad

    pieces, bias_pieces = lax.map(backward, (starts, feat_blocks))
    grad_dictionary = jnp.transpose(pieces, (1, 0, 2)).reshape(2, D, LATENTS)
    grad_bias = bias_pieces.reshape(LATENTS)
    return grad_dictionary, grad_bias
```

```python
import jax
import jax.numpy as jnp
from jax import lax
from jax.experimental import pallas as pl
from jax.experimental.pallas import tpu as pltpu
from jax.sharding import PartitionSpec as P

MESH = pl.DeviceIdType.MESH
F32 = jnp.float32
BF16 = jnp.bfloat16
NX, NZ, NY = 2, 8, 4
ROWS = 16
CHUNK = NZ * ROWS
FEAT = 512
LAT = 512
SENDS = 101


def nt_dot(left, right):
    return lax.dot_general(left, right, (((1,), (1,)), ((), ())), preferred_element_type=F32)


def tn_dot(left, right):
    return lax.dot_general(left, right, (((0,), (0,)), ((), ())), preferred_element_type=F32)


def step_kernel(
    attn, proj, resid, dict_hbm, bias, act,
    fields, errors, feats, gpre,
    dic, dic_sem, res_out, res_in,
    proj_acc, proj_out, proj_in, fold_out, fold_in,
    pre, half_out, half_in, pair_out, pair_in,
    rec_out, rec_own, x_in, y_out, y_in, z_out, z_in,
    sq_in, sz_out, sz_in, sx_out, sx_in,
    send_sem, recv_sem,
):
    wide = lax.axis_index("wide")
    narrow = lax.axis_index("narrow")
    xh, z, y = wide // 32, (wide // 4) % 8, wide % 4
    xl, core = narrow // 2, narrow % 2

    def dev(xh_=xh, z_=z, y_=y, xl_=xl, core_=core):
        return ((xh_ * 8 + z_) * 4 + y_, xl_ * 2 + core_)

    x_peer = dev(xh_=1 - xh)
    pair_peer = dev(xl_=1 - xl)
    core_peer = dev(core_=1 - core)
    y_at = [(y + k) % 4 for k in range(4)]
    z_at = [(z + k) % 8 for k in range(8)]
    y_peer = [dev(y_=at) for at in y_at]
    z_peer = [dev(z_=at) for at in z_at]

    dict_copy = pltpu.make_async_copy(dict_hbm, dic, dic_sem)
    dict_copy.start()

    barrier = pltpu.get_barrier_semaphore()
    partners = [x_peer, pair_peer, core_peer] + y_peer[1:] + z_peer[1:]
    for peer in partners:
        pl.semaphore_signal(barrier, inc=1, device_id=peer, device_id_type=MESH)
    pl.semaphore_wait(barrier, len(partners))

    started = []

    def send(src, dst, peer):
        slot = len(started)
        copy = pltpu.make_async_remote_copy(
            src_ref=src, dst_ref=dst, send_sem=send_sem.at[slot], recv_sem=recv_sem.at[slot],
            device_id=peer, device_id_type=MESH,
        )
        copy.start()
        started.append(copy)
        return copy

    for k in range(4):
        at = y_at[k]
        cols = pl.ds(pl.multiple_of(at * FEAT, FEAT), FEAT)
        if k == 0:
            res_in[0] = resid[:, cols].astype(F32)
        else:
            res_out[k] = resid[:, cols].astype(F32)
    res_copies = [send(res_out.at[k], res_in.at[k], y_peer[k]) for k in range(1, 4)]
    res_waited = []

    def gather(ref, c, first):
        if first == "z":
            copies = [send(ref.at[xh, y, c, z], ref.at[xh, y, c, z], z_peer[k]) for k in range(1, 8)]
            yield
            for copy in copies:
                copy.wait_recv()
            copies = [send(ref.at[xh, y, c], ref.at[xh, y, c], y_peer[k]) for k in range(1, 4)]
            yield
            for copy in copies:
                copy.wait_recv()
            copy = send(ref.at[xh, :, c], ref.at[xh, :, c], x_peer)
            yield
            copy.wait_recv()
        else:
            copy = send(ref.at[xh, y, c, z], ref.at[xh, y, c, z], x_peer)
            yield
            copy.wait_recv()
            copies = [send(ref.at[:, y, c, z], ref.at[:, y, c, z], z_peer[k]) for k in range(1, 8)]
            yield
            for copy in copies:
                copy.wait_recv()
            copies = [send(ref.at[:, y, c], ref.at[:, y, c], y_peer[k]) for k in range(1, 4)]
            yield
            for copy in copies:
                copy.wait_recv()

    def encode(ref, c, result, stage, with_bias):
        pre[c, stage] = jnp.zeros((CHUNK, LAT), F32)

        def block(j, _):
            rows = ref[j // NY, j % NY, c].reshape(CHUNK, FEAT)
            pre[c, stage] += jnp.dot(rows, dic[j], preferred_element_type=F32)
            return 0

        lax.fori_loop(0, NX * NY, block, 0)
        mine = pl.ds(pl.multiple_of(core * 64, 64), 64)
        theirs = pl.ds(pl.multiple_of((1 - core) * 64, 64), 64)
        half_out[c, stage] = pre[c, stage, theirs, :].astype(BF16)
        copy = send(half_out.at[c, stage], half_in.at[c, stage], core_peer)
        yield
        copy.wait_recv()
        half = (pre[c, stage, mine, :] + half_in[c, stage].astype(F32)).astype(BF16)
        pair_out[c, stage] = half
        copy = send(pair_out.at[c, stage], pair_in.at[c, stage], pair_peer)
        yield
        copy.wait_recv()
        total = pair_out[c, stage].astype(F32) + pair_in[c, stage].astype(F32)
        if with_bias:
            total = total + bias[...]
        places = pl.ds(core * 4, 4)
        mask = act[places, c].reshape(64, LAT).astype(F32)
        result[c, places] = (mask * total).astype(BF16).reshape(4, ROWS, LAT)
        copy = send(result.at[c, places], result.at[c, places], core_peer)
        yield
        copy.wait_recv()

    def chain(c):
        rows = attn[:, c].reshape(CHUNK, 256)
        copies = []
        for k in (1, 3, 2, 0):
            cols = pl.ds(pl.multiple_of(y_at[k] * FEAT, FEAT), FEAT)
            part = jnp.dot(rows, proj[:, cols], preferred_element_type=F32).reshape(NZ, ROWS, FEAT)
            if k == 0:
                proj_acc[c] = part
            else:
                proj_out[c, k] = part.astype(BF16)
                copies.append(send(proj_out.at[c, k], proj_in.at[c, k], y_peer[k]))
        yield
        for copy in copies:
            copy.wait_recv()
        summed = proj_acc[c]
        for k in range(1, 4):
            summed = summed + proj_in[c, k].astype(F32)
        proj_acc[c] = summed
        fold_out[c] = summed.astype(BF16)
        copies = [send(fold_out.at[c, z_at[k]], fold_in.at[c, k], z_peer[k]) for k in range(1, 8)]
        yield
        if not res_waited:
            for copy in res_copies:
                copy.wait_recv()
            res_waited.append(True)
        for copy in copies:
            copy.wait_recv()
        own = proj_acc[c, z]
        for k in range(1, 8):
            own = own + fold_in[c, k].astype(F32)
        low = res_in[(y - 2 * c + 4) % 4]
        high = res_in[(y - 2 * c + 3) % 4]
        fields[xh, y, c, z] = (own + jnp.concatenate([low, high], axis=0)).astype(BF16)
        yield from gather(fields, c, "z" if c == 0 else "x")
        if c == 0:
            dict_copy.wait()
        yield from encode(fields, c, feats, 0, True)

        code = feats[c].reshape(CHUNK, LAT)
        if c == 0:
            def other(j, _):
                rec_out[0, j] = nt_dot(code, dic[(1 - xh) * NY + j]).astype(BF16).reshape(NZ, ROWS, FEAT)
                return 0

            lax.fori_loop(0, NY, other, 0)
            copy = send(rec_out.at[0, pl.ds(0, 4)], x_in, x_peer)

            def mine(j, _):
                rec_own[0, j] = nt_dot(code, dic[xh * NY + j]).reshape(NZ, ROWS, FEAT)
                return 0

            lax.fori_loop(0, NY, mine, 0)
            yield
            copy.wait_recv()
            copies = []
            for k in (1, 3, 2, 0):
                at = y_at[k]
                part = rec_own[0, at] + x_in[at].astype(F32)
                if k == 0:
                    rec_own[0, at] = part
                else:
                    y_out[k] = part.astype(BF16)
                    copies.append(send(y_out.at[k], y_in.at[k], y_peer[k]))
            yield
            for copy in copies:
                copy.wait_recv()
            part = rec_own[0, y]
            for k in range(1, 4):
                part = part + y_in[k].astype(F32)
            rec_own[0, y] = part
            z_out[...] = part.astype(BF16)
            copies = [send(z_out.at[z_at[k]], z_in.at[k], z_peer[k]) for k in range(1, 8)]
            yield
            for copy in copies:
                copy.wait_recv()
            recon = rec_own[0, y, z]
            for k in range(1, 8):
                recon = recon + z_in[k].astype(F32)
        else:
            copies = []
            for k in (1, 3, 2, 0):
                at = y_at[k]
                for m in range(NX):
                    part = nt_dot(code, dic[m * NY + at]).reshape(NZ, ROWS, FEAT)
                    if k == 0:
                        rec_own[1, m] = part
                    else:
                        rec_out[1, 2 * (k - 1) + m] = part.astype(BF16)
                if k:
                    copies.append(send(rec_out.at[1, pl.ds(2 * (k - 1), 2)], sq_in.at[k], y_peer[k]))
            yield
            for copy in copies:
                copy.wait_recv()
            for m in range(NX):
                part = rec_own[1, m]
                for k in range(1, 4):
                    part = part + sq_in[k, m].astype(F32)
                rec_own[1, m] = part
                sz_out[m] = part.astype(BF16)
            copies = [send(sz_out.at[:, z_at[k]], sz_in.at[k], z_peer[k]) for k in range(1, 8)]
            yield
            for copy in copies:
                copy.wait_recv()
            part = rec_own[1, 1 - xh, z]
            for k in range(1, 8):
                part = part + sz_in[k, 1 - xh].astype(F32)
            sx_out[...] = part.astype(BF16)
            copy = send(sx_out, sx_in, x_peer)
            recon = rec_own[1, xh, z]
            for k in range(1, 8):
                recon = recon + sz_in[k, xh].astype(F32)
            rec_own[1, 2, 0] = recon
            yield
            copy.wait_recv()
            recon = rec_own[1, 2, 0] + sx_in[...].astype(F32)
        errors[xh, y, c, z] = (recon - fields[xh, y, c, z].astype(F32)).astype(BF16)
        yield from gather(errors, c, "z" if c == 0 else "x")
        yield from encode(errors, c, gpre, 1, False)

    running = [chain(0), chain(1)]
    while running:
        for one in list(running):
            if next(one, "end") == "end":
                running.remove(one)
    for copy in started:
        copy.wait_send()


def gradient_kernel(fields, errors, feats, gpre, grad, bias_grad):
    code = feats[...]
    slope = gpre[...]
    grad[...] = (tn_dot(fields[...], slope) + tn_dot(errors[...], code)).astype(BF16)

    @pl.when(pl.program_id(0) == 0)
    def _():
        bias_grad[...] = jnp.sum(slope.astype(F32), axis=0, keepdims=True)


def body(attention, out_proj, residual, dictionary, enc_bias, active):
    vmem = pl.BlockSpec(memory_space=pltpu.VMEM)
    piece = (NX, NY, 2, NZ, ROWS, FEAT)
    code = (2, NZ, ROWS, LAT)
    shapes = [piece, piece, code, code]
    fields, errors, feats, gpre = pl.pallas_call(
        step_kernel,
        out_shape=[jax.ShapeDtypeStruct(s, BF16) for s in shapes],
        in_specs=[vmem, vmem, vmem, pl.BlockSpec(memory_space=pl.ANY), vmem, vmem],
        out_specs=[vmem] * 4,
        scratch_shapes=[
            pltpu.VMEM((NX * NY, FEAT, LAT), BF16),
            pltpu.SemaphoreType.DMA,
            pltpu.VMEM((4, 8, FEAT), F32),
            pltpu.VMEM((4, 8, FEAT), F32),
            pltpu.VMEM((2, NZ, ROWS, FEAT), F32),
            pltpu.VMEM((2, 4, NZ, ROWS, FEAT), BF16),
            pltpu.VMEM((2, 4, NZ, ROWS, FEAT), BF16),
            pltpu.VMEM((2, NZ, ROWS, FEAT), BF16),
            pltpu.VMEM((2, 8, ROWS, FEAT), BF16),
            pltpu.VMEM((2, 2, CHUNK, LAT), F32),
            pltpu.VMEM((2, 2, 64, LAT), BF16),
            pltpu.VMEM((2, 2, 64, LAT), BF16),
            pltpu.VMEM((2, 2, 64, LAT), BF16),
            pltpu.VMEM((2, 2, 64, LAT), BF16),
            pltpu.VMEM((2, 6, NZ, ROWS, FEAT), BF16),
            pltpu.VMEM((2, 4, NZ, ROWS, FEAT), F32),
            pltpu.VMEM((4, NZ, ROWS, FEAT), BF16),
            pltpu.VMEM((4, NZ, ROWS, FEAT), BF16),
            pltpu.VMEM((4, NZ, ROWS, FEAT), BF16),
            pltpu.VMEM((NZ, ROWS, FEAT), BF16),
            pltpu.VMEM((8, ROWS, FEAT), BF16),
            pltpu.VMEM((4, 2, NZ, ROWS, FEAT), BF16),
            pltpu.VMEM((2, NZ, ROWS, FEAT), BF16),
            pltpu.VMEM((8, 2, ROWS, FEAT), BF16),
            pltpu.VMEM((ROWS, FEAT), BF16),
            pltpu.VMEM((ROWS, FEAT), BF16),
            pltpu.SemaphoreType.DMA((SENDS,)),
            pltpu.SemaphoreType.DMA((SENDS,)),
        ],
        compiler_params=pltpu.CompilerParams(
            collective_id=0, has_side_effects=True, vmem_limit_bytes=48 << 20
        ),
        name="crosscoder_step",
    )(
        attention.reshape(NZ, 2, ROWS, 256),
        out_proj,
        residual,
        dictionary.reshape(NX * NY, FEAT, LAT),
        enc_bias.reshape(1, LAT),
        active.reshape(NZ, 2, ROWS, LAT),
    )
    block = pl.BlockSpec((None, 2 * CHUNK, FEAT), lambda j: (j, 0, 0))
    whole = pl.BlockSpec((2 * CHUNK, LAT), lambda j: (0, 0))
    grad, bias_grad = pl.pallas_call(
        gradient_kernel,
        grid=(NX * NY,),
        out_shape=[
            jax.ShapeDtypeStruct((NX * NY, FEAT, LAT), BF16),
            jax.ShapeDtypeStruct((1, LAT), F32),
        ],
        in_specs=[block, block, whole, whole],
        out_specs=[
            pl.BlockSpec((None, FEAT, LAT), lambda j: (j, 0, 0)),
            pl.BlockSpec((1, LAT), lambda j: (0, 0)),
        ],
        compiler_params=pltpu.CompilerParams(vmem_limit_bytes=32 << 20),
        name="dictionary_gradient",
    )(
        fields.reshape(NX * NY, 2 * CHUNK, FEAT),
        errors.reshape(NX * NY, 2 * CHUNK, FEAT),
        feats.reshape(2 * CHUNK, LAT),
        gpre.reshape(2 * CHUNK, LAT),
    )
    return grad.reshape(dictionary.shape), bias_grad.reshape(LAT)


def solution(mesh):
    in_specs = (
        P(None, "wide"),
        P("wide", "narrow"),
        P("wide", "narrow"),
        P(None, "narrow", "wide"),
        P("wide"),
        P(None, "wide"),
    )
    out_specs = (P(None, "narrow", "wide"), P("wide"))
    return jax.shard_map(body, mesh=mesh, in_specs=in_specs, out_specs=out_specs, check_vma=False)
```

```python
import jax
import jax.numpy as jnp
from jax import lax
from jax.experimental import pallas as pl
from jax.experimental.pallas import tpu as pltpu
from jax.sharding import PartitionSpec as P

MESH = pl.DeviceIdType.MESH
F32 = jnp.float32
BF16 = jnp.bfloat16
NX, NZ, NY = 2, 8, 4
ROWS = 16
CHUNK = NZ * ROWS
FEAT = 512
LAT = 512
SENDS = 125
HALF = 256
DELAY = 1


def nt_dot(left, right):
    return lax.dot_general(left, right, (((1,), (1,)), ((), ())), preferred_element_type=F32)


def tn_dot(left, right):
    return lax.dot_general(left, right, (((0,), (0,)), ((), ())), preferred_element_type=F32)


def step_kernel(
    attn_hbm, proj_hbm, resid_hbm, dict_hbm, bias_hbm, act_hbm,
    turned_hbm, feats_hbm, gpre_hbm,
    turned, attn, proj, resid, dic, bias, act, fields, errors, feats, gpre,
    res_out, res_in,
    proj_acc, proj_out, proj_in, fold_out, fold_in,
    pre, half_out, half_in, pair_out, pair_in,
    xa_out, xa_in, xa_own, ya_out, ya_in,
    yb_out, yb_in, yb_own, xb_out, xb_in,
    z_own, z_out, z_in,
    local_sem, send_sem, recv_sem,
):
    wide = lax.axis_index("wide")
    narrow = lax.axis_index("narrow")
    xh, z, y = wide // 32, (wide // 4) % 8, wide % 4
    xl, core = narrow // 2, narrow % 2

    def dev(xh_=xh, z_=z, y_=y, xl_=xl, core_=core):
        return ((xh_ * 8 + z_) * 4 + y_, xl_ * 2 + core_)

    x_peer = dev(xh_=1 - xh)
    pair_peer = dev(xl_=1 - xl)
    core_peer = dev(core_=1 - core)
    y_at = [(y + k) % 4 for k in range(4)]
    z_at = [(z + k) % 8 for k in range(8)]
    y_peer = [dev(y_=at) for at in y_at]
    z_peer = [dev(z_=at) for at in z_at]

    barrier = pltpu.get_barrier_semaphore()
    partners = [x_peer, pair_peer, core_peer] + y_peer[1:] + z_peer[1:]
    for peer in partners:
        pl.semaphore_signal(barrier, inc=1, device_id=peer, device_id_type=MESH)

    loads = []
    for src, dst in (
        (attn_hbm, attn), (proj_hbm, proj), (resid_hbm, resid),
        (bias_hbm, bias), (act_hbm, act), (dict_hbm, dic),
    ):
        copy = pltpu.make_async_copy(src, dst, local_sem.at[len(loads)])
        copy.start()
        loads.append(copy)

    started = []
    stores = []

    def send(src, dst, peer):
        slot = len(started)
        copy = pltpu.make_async_remote_copy(
            src_ref=src, dst_ref=dst, send_sem=send_sem.at[slot], recv_sem=recv_sem.at[slot],
            device_id=peer, device_id_type=MESH,
        )
        copy.start()
        started.append(copy)
        return copy

    def store(src, dst):
        copy = pltpu.make_async_copy(src, dst, local_sem.at[len(loads) + len(stores)])
        copy.start()
        stores.append(copy)

    low, high = pl.ds(0, HALF), pl.ds(HALF, HALF)
    z_order = (4, 3, 5, 2, 6, 1, 7)
    y_order = (2, 1, 3)

    def gather(ref, c):
        copies = [send(ref.at[xh, y, c, z], ref.at[xh, y, c, z], z_peer[k]) for k in z_order]
        yield
        for copy in copies:
            copy.wait_recv()
        along = ref.at[xh, y, c, :, :, high]
        copies = [send(along, along, x_peer)]
        along = ref.at[xh, y, c, :, :, low]
        copies += [send(along, along, y_peer[k]) for k in y_order]
        yield
        for copy in copies[1:]:
            copy.wait_recv()
        along = ref.at[xh, :, c, :, :, low]
        last = [send(along, along, x_peer)]
        copies[0].wait_recv()
        along = ref.at[:, y, c, :, :, high]
        last += [send(along, along, y_peer[k]) for k in y_order]
        yield
        for copy in last:
            copy.wait_recv()

    def turn(ref, c, stage, blocks):
        for j in blocks:
            turned[stage, c, j] = ref[j // NY, j % NY, c].reshape(CHUNK, FEAT).T

    def encode(ref, c, result, stage, with_bias):
        total = None
        for m in range(NX):
            for at in range(NY):
                part = jnp.dot(ref[m, at, c].reshape(CHUNK, FEAT), dic[m * NY + at], preferred_element_type=F32)
                total = part if total is None else total + part
        pre[c, stage] = total
        mine = pl.ds(pl.multiple_of(core * 64, 64), 64)
        theirs = pl.ds(pl.multiple_of((1 - core) * 64, 64), 64)
        half_out[c, stage] = pre[c, stage, theirs, :].astype(BF16)
        copy = send(half_out.at[c, stage], half_in.at[c, stage], core_peer)
        turn(ref, c, stage, (0, 1))
        yield
        copy.wait_recv()
        half = (pre[c, stage, mine, :] + half_in[c, stage].astype(F32)).astype(BF16)
        pair_out[c, stage] = half
        copy = send(pair_out.at[c, stage], pair_in.at[c, stage], pair_peer)
        turn(ref, c, stage, range(2, NX * NY))
        store(turned.at[stage, c], turned_hbm.at[stage, c])
        yield
        copy.wait_recv()
        total = pair_out[c, stage].astype(F32) + pair_in[c, stage].astype(F32)
        if with_bias:
            total = total + bias[...]
        places = pl.ds(core * 4, 4)
        mask = act[places, c].reshape(64, LAT).astype(F32)
        result[c, places] = (mask * total).astype(BF16).reshape(4, ROWS, LAT)
        copy = send(result.at[c, places], result.at[c, places], core_peer)
        yield
        copy.wait_recv()

    def project(c):
        rows = attn[:, c].reshape(CHUNK, 256)
        for k in y_order + (0,):
            cols = pl.ds(pl.multiple_of(y_at[k] * FEAT, FEAT), FEAT)
            part = jnp.dot(rows, proj[:, cols], preferred_element_type=F32).reshape(NZ, ROWS, FEAT)
            if k == 0:
                proj_acc[c] = part
            else:
                proj_out[c, k] = part.astype(BF16)

    def chain(c):
        copies = [send(proj_out.at[c, k], proj_in.at[c, k], y_peer[k]) for k in y_order]
        yield
        for copy in copies:
            copy.wait_recv()
        summed = proj_acc[c]
        for k in range(1, 4):
            summed = summed + proj_in[c, k].astype(F32)
        proj_acc[c] = summed
        fold_out[c] = summed.astype(BF16)
        copies = [send(fold_out.at[c, z_at[k]], fold_in.at[c, k], z_peer[k]) for k in z_order]
        yield
        if c == 0:
            for copy in res_copies:
                copy.wait_recv()
        for copy in copies:
            copy.wait_recv()
        own = proj_acc[c, z]
        for k in range(1, 8):
            own = own + fold_in[c, k].astype(F32)
        upper = res_in[(y - 2 * c + 4) % 4]
        lower = res_in[(y - 2 * c + 3) % 4]
        fields[xh, y, c, z] = (own + jnp.concatenate([upper, lower], axis=0)).astype(BF16)
        yield from gather(fields, c)
        if c == 0:
            for copy in loads[3:]:
                copy.wait()
        yield from encode(fields, c, feats, 0, True)
        store(feats.at[c], feats_hbm.at[c])

        code = feats[c].reshape(CHUNK, LAT)

        def decode(j, cols):
            return nt_dot(code, dic[j, cols, :]).reshape(NZ, ROWS, HALF)

        for at in range(NY):
            xa_out[c, at] = decode((1 - xh) * NY + at, low).astype(BF16)
        xa_copy = send(xa_out.at[c], xa_in.at[c], x_peer)
        yb_copies = []
        for k in y_order:
            for m in range(NX):
                yb_out[c, k, m] = decode(m * NY + y_at[k], high).astype(BF16)
            yb_copies.append(send(yb_out.at[c, k], yb_in.at[c, k], y_peer[k]))
        for at in range(NY):
            xa_own[c, at] = decode(xh * NY + at, low)
        for m in range(NX):
            yb_own[c, m] = decode(m * NY + y, high)
        yield
        xa_copy.wait_recv()
        ya_copies = []
        for k in y_order + (0,):
            at = y_at[k]
            part = xa_own[c, at] + xa_in[c, at].astype(F32)
            if k == 0:
                z_own[c, :, :, :HALF] = part
            else:
                ya_out[c, k] = part.astype(BF16)
                ya_copies.append(send(ya_out.at[c, k], ya_in.at[c, k], y_peer[k]))
        for copy in yb_copies:
            copy.wait_recv()

        def over_y(m):
            part = yb_own[c, m]
            for k in range(1, 4):
                part = part + yb_in[c, k, m].astype(F32)
            return part

        xb_out[c] = over_y(1 - xh).astype(BF16)
        xb_copy = send(xb_out.at[c], xb_in.at[c], x_peer)
        z_own[c, :, :, HALF:] = over_y(xh)
        yield
        for copy in ya_copies:
            copy.wait_recv()
        part = z_own[c, :, :, :HALF]
        for k in range(1, 4):
            part = part + ya_in[c, k].astype(F32)
        z_own[c, :, :, :HALF] = part
        z_out[c, :, :, :HALF] = part.astype(BF16)
        xb_copy.wait_recv()
        part = z_own[c, :, :, HALF:] + xb_in[c].astype(F32)
        z_own[c, :, :, HALF:] = part
        z_out[c, :, :, HALF:] = part.astype(BF16)
        copies = [send(z_out.at[c, z_at[k]], z_in.at[c, k], z_peer[k]) for k in z_order]
        yield
        for copy in copies:
            copy.wait_recv()
        recon = z_own[c, z]
        for k in range(1, 8):
            recon = recon + z_in[c, k].astype(F32)
        errors[xh, y, c, z] = (recon - fields[xh, y, c, z].astype(F32)).astype(BF16)
        yield from gather(errors, c)
        yield from encode(errors, c, gpre, 1, False)
        store(gpre.at[c], gpre_hbm.at[c])

    for copy in loads[:2]:
        copy.wait()
    project(0)
    loads[2].wait()
    for k in range(4):
        cols = pl.ds(pl.multiple_of(y_at[k] * FEAT, FEAT), FEAT)
        if k == 0:
            res_in[0] = resid[:, cols].astype(F32)
        else:
            res_out[k] = resid[:, cols].astype(F32)
    pl.semaphore_wait(barrier, len(partners))
    first, second = chain(0), chain(1)
    next(first)
    res_copies = [send(res_out.at[k], res_in.at[k], y_peer[k]) for k in y_order]
    project(1)
    for _ in range(DELAY):
        next(first)
    running = [second, first]
    while running:
        for one in list(running):
            if next(one, "end") == "end":
                running.remove(one)
    for copy in started:
        copy.wait_send()
    for copy in stores:
        copy.wait()


def gradient_kernel(
    turned_hbm, feats_hbm, gpre_hbm, grad_hbm, bias_grad, turned, code, grad, code_sem, in_sem, out_sem
):
    first = [
        pltpu.make_async_copy(gpre_hbm, code.at[0], code_sem.at[0]),
        pltpu.make_async_copy(feats_hbm, code.at[1], code_sem.at[1]),
    ]
    blocks = [
        pltpu.make_async_copy(turned_hbm.at[:, :, j], turned.at[:, :, j], in_sem.at[j]) for j in range(NX * NY)
    ]
    for copy in first + blocks:
        copy.start()
    for copy in first:
        copy.wait()
    right = code[...].reshape(4 * CHUNK, LAT)
    stores = []
    for j in range(NX * NY):
        blocks[j].wait()
        left = jnp.concatenate([turned[s, c, j] for s in range(2) for c in range(2)], axis=1)
        grad[j] = jnp.dot(left, right, preferred_element_type=F32).astype(BF16)
        copy = pltpu.make_async_copy(grad.at[j], grad_hbm.at[j], out_sem.at[j])
        copy.start()
        stores.append(copy)
    bias_grad[...] = jnp.sum(code[0].astype(F32).reshape(2 * CHUNK, LAT), axis=0, keepdims=True)
    for copy in stores:
        copy.wait()


def body(attention, out_proj, residual, dictionary, enc_bias, active):
    hbm = pl.BlockSpec(memory_space=pl.ANY)
    piece = (NX, NY, 2, NZ, ROWS, FEAT)
    code = (2, NZ, ROWS, LAT)
    half = (NZ, ROWS, HALF)
    flipped = (2, 2, NX * NY, FEAT, CHUNK)
    shapes = [flipped, code, code]
    turned, feats, gpre = pl.pallas_call(
        step_kernel,
        out_shape=[jax.ShapeDtypeStruct(s, BF16) for s in shapes],
        in_specs=[hbm] * 6,
        out_specs=[hbm] * 3,
        scratch_shapes=[
            pltpu.VMEM(flipped, BF16),
            pltpu.VMEM((NZ, 2, ROWS, 256), BF16),
            pltpu.VMEM((256, NY * FEAT), BF16),
            pltpu.VMEM((8, NY * FEAT), BF16),
            pltpu.VMEM((NX * NY, FEAT, LAT), BF16),
            pltpu.VMEM((1, LAT), F32),
            pltpu.VMEM((NZ, 2, ROWS, LAT), jnp.int32),
            pltpu.VMEM(piece, BF16),
            pltpu.VMEM(piece, BF16),
            pltpu.VMEM(code, BF16),
            pltpu.VMEM(code, BF16),
            pltpu.VMEM((4, 8, FEAT), F32),
            pltpu.VMEM((4, 8, FEAT), F32),
            pltpu.VMEM((2, NZ, ROWS, FEAT), F32),
            pltpu.VMEM((2, 4, NZ, ROWS, FEAT), BF16),
            pltpu.VMEM((2, 4, NZ, ROWS, FEAT), BF16),
            pltpu.VMEM((2, NZ, ROWS, FEAT), BF16),
            pltpu.VMEM((2, 8, ROWS, FEAT), BF16),
            pltpu.VMEM((2, 2, CHUNK, LAT), F32),
            pltpu.VMEM((2, 2, 64, LAT), BF16),
            pltpu.VMEM((2, 2, 64, LAT), BF16),
            pltpu.VMEM((2, 2, 64, LAT), BF16),
            pltpu.VMEM((2, 2, 64, LAT), BF16),
            pltpu.VMEM((2, NY) + half, BF16),
            pltpu.VMEM((2, NY) + half, BF16),
            pltpu.VMEM((2, NY) + half, F32),
            pltpu.VMEM((2, 4) + half, BF16),
            pltpu.VMEM((2, 4) + half, BF16),
            pltpu.VMEM((2, 4, NX) + half, BF16),
            pltpu.VMEM((2, 4, NX) + half, BF16),
            pltpu.VMEM((2, NX) + half, F32),
            pltpu.VMEM((2,) + half, BF16),
            pltpu.VMEM((2,) + half, BF16),
            pltpu.VMEM((2, NZ, ROWS, FEAT), F32),
            pltpu.VMEM((2, NZ, ROWS, FEAT), BF16),
            pltpu.VMEM((2, 8, ROWS, FEAT), BF16),
            pltpu.SemaphoreType.DMA((14,)),
            pltpu.SemaphoreType.DMA((SENDS,)),
            pltpu.SemaphoreType.DMA((SENDS,)),
        ],
        compiler_params=pltpu.CompilerParams(
            collective_id=0, has_side_effects=True, vmem_limit_bytes=60 << 20
        ),
        name="crosscoder_step",
    )(
        attention.reshape(NZ, 2, ROWS, 256),
        out_proj,
        residual,
        dictionary.reshape(NX * NY, FEAT, LAT),
        enc_bias.reshape(1, LAT),
        active.reshape(NZ, 2, ROWS, LAT),
    )
    grad, bias_grad = pl.pallas_call(
        gradient_kernel,
        out_shape=[
            jax.ShapeDtypeStruct((NX * NY, FEAT, LAT), BF16),
            jax.ShapeDtypeStruct((1, LAT), F32),
        ],
        in_specs=[hbm] * 3,
        out_specs=[hbm, pl.BlockSpec(memory_space=pltpu.VMEM)],
        scratch_shapes=[
            pltpu.VMEM(flipped, BF16),
            pltpu.VMEM((2,) + code, BF16),
            pltpu.VMEM((NX * NY, FEAT, LAT), BF16),
            pltpu.SemaphoreType.DMA((2,)),
            pltpu.SemaphoreType.DMA((NX * NY,)),
            pltpu.SemaphoreType.DMA((NX * NY,)),
        ],
        compiler_params=pltpu.CompilerParams(vmem_limit_bytes=60 << 20),
        name="dictionary_gradient",
    )(turned, feats, gpre)
    return grad.reshape(dictionary.shape), bias_grad.reshape(LAT)


def solution(mesh):
    in_specs = (
        P(None, "wide"),
        P("wide", "narrow"),
        P("wide", "narrow"),
        P(None, "narrow", "wide"),
        P("wide"),
        P(None, "wide"),
    )
    out_specs = (P(None, "narrow", "wide"), P("wide"))
    return jax.shard_map(body, mesh=mesh, in_specs=in_specs, out_specs=out_specs, check_vma=False)
```

```python
import jax
import jax.numpy as jnp
from jax import lax
from jax.experimental import pallas as pl
from jax.experimental.pallas import tpu as pltpu
from jax.sharding import PartitionSpec as P

MESH = pl.DeviceIdType.MESH
F32 = jnp.float32
BF16 = jnp.bfloat16
NX, NZ, NY = 2, 8, 4
ROWS = 16
CHUNK = NZ * ROWS
FEAT = 512
LAT = 512
SENDS = 47
LATE = 46
HALF = 256
DELAY = 1


def nt_dot(left, right):
    return lax.dot_general(left, right, (((1,), (1,)), ((), ())), preferred_element_type=F32)


def tn_dot(left, right):
    return lax.dot_general(left, right, (((0,), (0,)), ((), ())), preferred_element_type=F32)


def step_kernel(
    attn_hbm, proj_hbm, resid_hbm, dict_hbm, bias_hbm, act_hbm,
    turned_hbm, feats_hbm, gpre_hbm,
    turned, attn, proj, resid, dic, bias, act, fields, errors, feats, gpre,
    res_out, res_in,
    proj_acc, proj_out, proj_in, fold_out, fold_in,
    pre, half_out, half_in, pair_out, pair_in,
    xa_out, xa_in, xa_own, ya_out, ya_in,
    yb_out, yb_in, yb_own, xb_out, xb_in,
    z_own, z_out, z_in,
    local_sem, send_sem, recv_sem,
):
    wide = lax.axis_index("wide")
    narrow = lax.axis_index("narrow")
    xh, z, y = wide // 32, (wide // 4) % 8, wide % 4
    xl, core = narrow // 2, narrow % 2

    def dev(xh_=xh, z_=z, y_=y, xl_=xl, core_=core):
        return ((xh_ * 8 + z_) * 4 + y_, xl_ * 2 + core_)

    x_peer = dev(xh_=1 - xh)
    pair_peer = dev(xl_=1 - xl)
    core_peer = dev(core_=1 - core)
    y_at = [(y + k) % 4 for k in range(4)]
    z_at = [(z + k) % 8 for k in range(8)]
    y_peer = [dev(y_=at) for at in y_at]
    z_peer = [dev(z_=at) for at in z_at]

    barrier = pltpu.get_barrier_semaphore()
    partners = [x_peer, pair_peer, core_peer] + y_peer[1:] + z_peer[1:]
    for peer in partners:
        pl.semaphore_signal(barrier, inc=1, device_id=peer, device_id_type=MESH)

    loads = []
    for src, dst in (
        (attn_hbm, attn), (proj_hbm, proj), (resid_hbm, resid),
        (bias_hbm, bias), (act_hbm, act), (dict_hbm, dic),
    ):
        copy = pltpu.make_async_copy(src, dst, local_sem.at[len(loads)])
        copy.start()
        loads.append(copy)

    groups = []
    stores = []

    class Group:
        def __init__(self, size, copies):
            slot = len(groups)
            self.size, self.sems, self.sent = size, (send_sem.at[slot], recv_sem.at[slot]), False
            for src, dst, peer in copies:
                pltpu.make_async_remote_copy(
                    src_ref=src, dst_ref=dst, send_sem=self.sems[0], recv_sem=self.sems[1],
                    device_id=peer, device_id_type=MESH,
                ).start()
            groups.append(self)

        def wait_recv(self):
            pltpu.make_async_copy(self.size, self.size, self.sems[1]).wait()

        def wait_send(self):
            if not self.sent:
                pltpu.make_async_copy(self.size, self.size, self.sems[0]).wait()
            self.sent = True

    def send(src, dst, peer):
        return Group(dst, [(src, dst, peer)])

    def along_y(src, dst, size):
        return Group(size, [(src(k), dst(k), y_peer[k]) for k in y_order])

    def along_z(src, dst, size):
        return Group(size, [(src(k), dst(k), z_peer[k]) for k in z_order])

    def store(src, dst):
        copy = pltpu.make_async_copy(src, dst, local_sem.at[len(loads) + len(stores)])
        copy.start()
        stores.append(copy)

    low, high = pl.ds(0, HALF), pl.ds(HALF, HALF)
    z_order = (4, 3, 5, 2, 6, 1, 7)
    y_order = (2, 1, 3)

    def gather(ref, c):
        own = ref.at[xh, y, c, z]
        group = along_z(lambda k: own, lambda k: own, ref.at[xh, y, c, pl.ds(0, 7)])
        yield
        group.wait_recv()
        own_high = ref.at[xh, y, c, :, :, high]
        own_low = ref.at[xh, y, c, :, :, low]
        over_y = along_y(lambda k: own_low, lambda k: own_low, ref.at[xh, pl.ds(0, 3), c, :, :, low])
        over_x = send(own_high, own_high, x_peer)
        yield
        over_y.wait_recv()
        all_low = ref.at[xh, :, c, :, :, low]
        last_x = send(all_low, all_low, x_peer)
        over_x.wait_recv()
        both_high = ref.at[:, y, c, :, :, high]
        last_y = along_y(lambda k: both_high, lambda k: both_high, ref.at[:, pl.ds(0, 3), c, :, :, high])
        yield
        last_x.wait_recv()
        last_y.wait_recv()

    def turn(ref, c, stage, blocks):
        for j in blocks:
            turned[stage, c, j] = ref[j // NY, j % NY, c].reshape(CHUNK, FEAT).T

    def encode(ref, c, result, stage, with_bias):
        total = None
        for m in range(NX):
            for at in range(NY):
                part = jnp.dot(ref[m, at, c].reshape(CHUNK, FEAT), dic[m * NY + at], preferred_element_type=F32)
                total = part if total is None else total + part
        pre[c, stage] = total
        mine = pl.ds(pl.multiple_of(core * 64, 64), 64)
        theirs = pl.ds(pl.multiple_of((1 - core) * 64, 64), 64)
        half_out[c, stage] = pre[c, stage, theirs, :].astype(BF16)
        copy = send(half_out.at[c, stage], half_in.at[c, stage], core_peer)
        turn(ref, c, stage, (0, 1))
        yield
        copy.wait_recv()
        half = (pre[c, stage, mine, :] + half_in[c, stage].astype(F32)).astype(BF16)
        pair_out[c, stage] = half
        copy = send(pair_out.at[c, stage], pair_in.at[c, stage], pair_peer)
        turn(ref, c, stage, range(2, NX * NY))
        store(turned.at[stage, c], turned_hbm.at[stage, c])
        yield
        copy.wait_recv()
        total = pair_out[c, stage].astype(F32) + pair_in[c, stage].astype(F32)
        if with_bias:
            total = total + bias[...]
        places = pl.ds(core * 4, 4)
        mask = act[places, c].reshape(64, LAT).astype(F32)
        result[c, places] = (mask * total).astype(BF16).reshape(4, ROWS, LAT)
        copy = send(result.at[c, places], result.at[c, places], core_peer)
        yield
        copy.wait_recv()

    def project(c):
        rows = attn[:, c].reshape(CHUNK, 256)
        for k in y_order + (0,):
            cols = pl.ds(pl.multiple_of(y_at[k] * FEAT, FEAT), FEAT)
            part = jnp.dot(rows, proj[:, cols], preferred_element_type=F32).reshape(NZ, ROWS, FEAT)
            if k == 0:
                proj_acc[c] = part
            else:
                proj_out[c, k] = part.astype(BF16)

    def chain(c):
        group = along_y(lambda k: proj_out.at[c, k], lambda k: proj_in.at[c, k], proj_in.at[c, pl.ds(1, 3)])
        yield
        group.wait_recv()
        summed = proj_acc[c]
        for k in range(1, 4):
            summed = summed + proj_in[c, k].astype(F32)
        proj_acc[c] = summed
        fold_out[c] = summed.astype(BF16)
        group = along_z(lambda k: fold_out.at[c, z_at[k]], lambda k: fold_in.at[c, k], fold_in.at[c, pl.ds(1, 7)])
        yield
        if c == 0:
            res_group.wait_recv()
        group.wait_recv()
        own = proj_acc[c, z]
        for k in range(1, 8):
            own = own + fold_in[c, k].astype(F32)
        upper = res_in[(y - 2 * c + 4) % 4]
        lower = res_in[(y - 2 * c + 3) % 4]
        fields[xh, y, c, z] = (own + jnp.concatenate([upper, lower], axis=0)).astype(BF16)
        yield from gather(fields, c)
        if c == 0:
            for copy in loads[3:]:
                copy.wait()
        yield from encode(fields, c, feats, 0, True)
        store(feats.at[c], feats_hbm.at[c])

        code = feats[c].reshape(CHUNK, LAT)

        def decode(j, cols):
            return nt_dot(code, dic[j, cols, :]).reshape(NZ, ROWS, HALF)

        for at in range(NY):
            xa_out[c, at] = decode((1 - xh) * NY + at, low).astype(BF16)
        xa_copy = send(xa_out.at[c], xa_in.at[c], x_peer)
        for k in y_order:
            for m in range(NX):
                yb_out[c, k, m] = decode(m * NY + y_at[k], high).astype(BF16)
        yb_group = along_y(lambda k: yb_out.at[c, k], lambda k: yb_in.at[c, k], yb_in.at[c, pl.ds(1, 3)])
        for at in range(NY):
            xa_own[c, at] = decode(xh * NY + at, low)
        for m in range(NX):
            yb_own[c, m] = decode(m * NY + y, high)
        yield
        xa_copy.wait_recv()
        for k in y_order + (0,):
            at = y_at[k]
            part = xa_own[c, at] + xa_in[c, at].astype(F32)
            if k == 0:
                z_own[c, :, :, :HALF] = part
            else:
                ya_out[c, k] = part.astype(BF16)
        ya_group = along_y(lambda k: ya_out.at[c, k], lambda k: ya_in.at[c, k], ya_in.at[c, pl.ds(1, 3)])
        yb_group.wait_recv()

        def over_y(m):
            part = yb_own[c, m]
            for k in range(1, 4):
                part = part + yb_in[c, k, m].astype(F32)
            return part

        xb_out[c] = over_y(1 - xh).astype(BF16)
        xb_copy = send(xb_out.at[c], xb_in.at[c], x_peer)
        z_own[c, :, :, HALF:] = over_y(xh)
        yield
        ya_group.wait_recv()
        part = z_own[c, :, :, :HALF]
        for k in range(1, 4):
            part = part + ya_in[c, k].astype(F32)
        z_own[c, :, :, :HALF] = part
        z_out[c, :, :, :HALF] = part.astype(BF16)
        xb_copy.wait_recv()
        part = z_own[c, :, :, HALF:] + xb_in[c].astype(F32)
        z_own[c, :, :, HALF:] = part
        z_out[c, :, :, HALF:] = part.astype(BF16)
        group = along_z(lambda k: z_out.at[c, z_at[k]], lambda k: z_in.at[c, k], z_in.at[c, pl.ds(1, 7)])
        yield
        group.wait_recv()
        recon = z_own[c, z]
        for k in range(1, 8):
            recon = recon + z_in[c, k].astype(F32)
        errors[xh, y, c, z] = (recon - fields[xh, y, c, z].astype(F32)).astype(BF16)
        yield from gather(errors, c)
        yield from encode(errors, c, gpre, 1, False)
        store(gpre.at[c], gpre_hbm.at[c])

    for copy in loads[:2]:
        copy.wait()
    project(0)
    loads[2].wait()
    for k in range(4):
        cols = pl.ds(pl.multiple_of(y_at[k] * FEAT, FEAT), FEAT)
        if k == 0:
            res_in[0] = resid[:, cols].astype(F32)
        else:
            res_out[k] = resid[:, cols].astype(F32)
    pl.semaphore_wait(barrier, len(partners))
    first, second = chain(0), chain(1)
    next(first)
    res_group = along_y(lambda k: res_out.at[k], lambda k: res_in.at[k], res_in.at[pl.ds(1, 3)])
    project(1)
    for _ in range(DELAY):
        next(first)
    running = [second, first]
    while running:
        for one in list(running):
            if next(one, "end") == "end":
                running.remove(one)
            for group in groups[:-LATE]:
                group.wait_send()
    for group in groups:
        group.wait_send()
    for copy in stores:
        copy.wait()


def gradient_kernel(turned, feats, gpre, grad_hbm, bias_grad, grad, out_sem):
    slope = gpre[...].reshape(2 * CHUNK, LAT)
    right = jnp.concatenate([slope, feats[...].reshape(2 * CHUNK, LAT)], axis=0)
    stores = []
    for j in range(NX * NY):
        left = jnp.concatenate([turned[s, c, j] for s in range(2) for c in range(2)], axis=1)
        grad[j] = jnp.dot(left, right, preferred_element_type=F32).astype(BF16)
        copy = pltpu.make_async_copy(grad.at[j], grad_hbm.at[j], out_sem.at[j])
        copy.start()
        stores.append(copy)
    bias_grad[...] = jnp.sum(slope.astype(F32), axis=0, keepdims=True)
    for copy in stores:
        copy.wait()


def body(attention, out_proj, residual, dictionary, enc_bias, active):
    hbm = pl.BlockSpec(memory_space=pl.ANY)
    vmem = pl.BlockSpec(memory_space=pltpu.VMEM)
    piece = (NX, NY, 2, NZ, ROWS, FEAT)
    code = (2, NZ, ROWS, LAT)
    half = (NZ, ROWS, HALF)
    flipped = (2, 2, NX * NY, FEAT, CHUNK)
    shapes = [flipped, code, code]
    turned, feats, gpre = pl.pallas_call(
        step_kernel,
        out_shape=[pltpu.VMEM(s, BF16) for s in shapes],
        in_specs=[pl.BlockSpec(memory_space=pltpu.HBM)] * 6,
        out_specs=[hbm] * 3,
        scratch_shapes=[
            pltpu.VMEM(flipped, BF16),
            pltpu.VMEM((NZ, 2, ROWS, 256), BF16),
            pltpu.VMEM((256, NY * FEAT), BF16),
            pltpu.VMEM((8, NY * FEAT), BF16),
            pltpu.VMEM((NX * NY, FEAT, LAT), BF16),
            pltpu.VMEM((1, LAT), F32),
            pltpu.VMEM((NZ, 2, ROWS, LAT), jnp.int32),
            pltpu.VMEM(piece, BF16),
            pltpu.VMEM(piece, BF16),
            pltpu.VMEM(code, BF16),
            pltpu.VMEM(code, BF16),
            pltpu.VMEM((4, 8, FEAT), F32),
            pltpu.VMEM((4, 8, FEAT), F32),
            pltpu.VMEM((2, NZ, ROWS, FEAT), F32),
            pltpu.VMEM((2, 4, NZ, ROWS, FEAT), BF16),
            pltpu.VMEM((2, 4, NZ, ROWS, FEAT), BF16),
            pltpu.VMEM((2, NZ, ROWS, FEAT), BF16),
            pltpu.VMEM((2, 8, ROWS, FEAT), BF16),
            pltpu.VMEM((2, 2, CHUNK, LAT), F32),
            pltpu.VMEM((2, 2, 64, LAT), BF16),
            pltpu.VMEM((2, 2, 64, LAT), BF16),
            pltpu.VMEM((2, 2, 64, LAT), BF16),
            pltpu.VMEM((2, 2, 64, LAT), BF16),
            pltpu.VMEM((2, NY) + half, BF16),
            pltpu.VMEM((2, NY) + half, BF16),
            pltpu.VMEM((2, NY) + half, F32),
            pltpu.VMEM((2, 4) + half, BF16),
            pltpu.VMEM((2, 4) + half, BF16),
            pltpu.VMEM((2, 4, NX) + half, BF16),
            pltpu.VMEM((2, 4, NX) + half, BF16),
            pltpu.VMEM((2, NX) + half, F32),
            pltpu.VMEM((2,) + half, BF16),
            pltpu.VMEM((2,) + half, BF16),
            pltpu.VMEM((2, NZ, ROWS, FEAT), F32),
            pltpu.VMEM((2, NZ, ROWS, FEAT), BF16),
            pltpu.VMEM((2, 8, ROWS, FEAT), BF16),
            pltpu.SemaphoreType.DMA((14,)),
            pltpu.SemaphoreType.DMA((SENDS,)),
            pltpu.SemaphoreType.DMA((SENDS,)),
        ],
        compiler_params=pltpu.CompilerParams(
            collective_id=0, has_side_effects=True, vmem_limit_bytes=50 << 20
        ),
        name="crosscoder_step",
    )(
        attention.reshape(NZ, 2, ROWS, 256),
        out_proj,
        residual,
        dictionary.reshape(NX * NY, FEAT, LAT),
        enc_bias.reshape(1, LAT),
        active.reshape(NZ, 2, ROWS, LAT),
    )
    grad, bias_grad = pl.pallas_call(
        gradient_kernel,
        out_shape=[
            jax.ShapeDtypeStruct((NX * NY, FEAT, LAT), BF16),
            jax.ShapeDtypeStruct((1, LAT), F32),
        ],
        in_specs=[vmem] * 3,
        out_specs=[hbm, vmem],
        scratch_shapes=[
            pltpu.VMEM((NX * NY, FEAT, LAT), BF16),
            pltpu.SemaphoreType.DMA((NX * NY,)),
        ],
        compiler_params=pltpu.CompilerParams(vmem_limit_bytes=24 << 20),
        name="dictionary_gradient",
    )(turned, feats, gpre)
    return grad.reshape(dictionary.shape), bias_grad.reshape(LAT)


def solution(mesh):
    in_specs = (
        P(None, "wide"),
        P("wide", "narrow"),
        P("wide", "narrow"),
        P(None, "narrow", "wide"),
        P("wide"),
        P(None, "wide"),
    )
    out_specs = (P(None, "narrow", "wide"), P("wide"))
    return jax.shard_map(body, mesh=mesh, in_specs=in_specs, out_specs=out_specs, check_vma=False)
```

```python
import jax
import jax.numpy as jnp
from jax import lax
from jax.experimental import pallas as pl
from jax.experimental.pallas import tpu as pltpu
from jax.sharding import PartitionSpec as P

MESH = pl.DeviceIdType.MESH
F32 = jnp.float32
BF16 = jnp.bfloat16
NX, NZ, NY = 2, 8, 4
ROWS = 16
CHUNK = NZ * ROWS
FEAT = 512
LAT = 512
SENDS = 47
HALF = 256
ORDER = "01010001100110011001101101010011100110011"


def nt_dot(left, right):
    return lax.dot_general(left, right, (((1,), (1,)), ((), ())), preferred_element_type=F32)


def tn_dot(left, right):
    return lax.dot_general(left, right, (((0,), (0,)), ((), ())), preferred_element_type=F32)


def step_kernel(
    attn_hbm, proj_hbm, resid_hbm, dict_hbm, bias_hbm, act_hbm,
    turned_hbm, feats_hbm, gpre_hbm,
    turned, attn, proj, resid, dic, bias, act, fields, errors, feats, gpre,
    res_out, res_in,
    proj_acc, proj_out, proj_in, fold_out, fold_in,
    pre, half_out, half_in, pair_out, pair_in,
    xa_out, xa_in, xa_own, ya_out, ya_in,
    yb_out, yb_in, yb_own, xb_out, xb_in,
    z_own, z_out, z_in,
    local_sem, send_sem, recv_sem,
):
    wide = lax.axis_index("wide")
    narrow = lax.axis_index("narrow")
    xh, z, y = wide // 32, (wide // 4) % 8, wide % 4
    xl, core = narrow // 2, narrow % 2

    def dev(xh_=xh, z_=z, y_=y, xl_=xl, core_=core):
        return ((xh_ * 8 + z_) * 4 + y_, xl_ * 2 + core_)

    x_peer = dev(xh_=1 - xh)
    pair_peer = dev(xl_=1 - xl)
    core_peer = dev(core_=1 - core)
    y_at = [(y + k) % 4 for k in range(4)]
    z_at = [(z + k) % 8 for k in range(8)]
    y_peer = [dev(y_=at) for at in y_at]
    z_peer = [dev(z_=at) for at in z_at]

    barrier = pltpu.get_barrier_semaphore()
    partners = [x_peer, pair_peer, core_peer] + y_peer[1:] + z_peer[1:]
    for peer in partners:
        pl.semaphore_signal(barrier, inc=1, device_id=peer, device_id_type=MESH)

    loads = []
    for src, dst in (
        (attn_hbm, attn), (proj_hbm, proj), (resid_hbm, resid),
        (bias_hbm, bias), (act_hbm, act), (dict_hbm, dic),
    ):
        copy = pltpu.make_async_copy(src, dst, local_sem.at[len(loads)])
        copy.start()
        loads.append(copy)

    groups = []
    stores = []

    class Group:
        def __init__(self, size, copies):
            slot = len(groups)
            self.size, self.sems, self.sent = size, (send_sem.at[slot], recv_sem.at[slot]), False
            for src, dst, peer in copies:
                pltpu.make_async_remote_copy(
                    src_ref=src, dst_ref=dst, send_sem=self.sems[0], recv_sem=self.sems[1],
                    device_id=peer, device_id_type=MESH,
                ).start()
            groups.append(self)

        def wait_recv(self):
            pltpu.make_async_copy(self.size, self.size, self.sems[1]).wait()

        def wait_send(self):
            if not self.sent:
                pltpu.make_async_copy(self.size, self.size, self.sems[0]).wait()
            self.sent = True

    def send(src, dst, peer):
        return Group(dst, [(src, dst, peer)])

    def along_y(src, dst, size):
        return Group(size, [(src(k), dst(k), y_peer[k]) for k in y_order])

    def along_z(src, dst, size):
        return Group(size, [(src(k), dst(k), z_peer[k]) for k in z_order])

    def store(src, dst):
        copy = pltpu.make_async_copy(src, dst, local_sem.at[len(loads) + len(stores)])
        copy.start()
        stores.append(copy)

    low, high = pl.ds(0, HALF), pl.ds(HALF, HALF)
    z_order = (4, 3, 5, 2, 6, 1, 7)
    y_order = (2, 1, 3)

    def gather(ref, c):
        own = ref.at[xh, y, c, z]
        group = along_z(lambda k: own, lambda k: own, ref.at[xh, y, c, pl.ds(0, 7)])
        yield
        group.wait_recv()
        own_high = ref.at[xh, y, c, :, :, high]
        own_low = ref.at[xh, y, c, :, :, low]
        over_y = along_y(lambda k: own_low, lambda k: own_low, ref.at[xh, pl.ds(0, 3), c, :, :, low])
        over_x = send(own_high, own_high, x_peer)
        yield
        over_y.wait_recv()
        all_low = ref.at[xh, :, c, :, :, low]
        last_x = send(all_low, all_low, x_peer)
        yield
        over_x.wait_recv()
        both_high = ref.at[:, y, c, :, :, high]
        last_y = along_y(lambda k: both_high, lambda k: both_high, ref.at[:, pl.ds(0, 3), c, :, :, high])
        yield
        last_x.wait_recv()
        last_y.wait_recv()

    def turn(ref, c, stage, blocks):
        for j in blocks:
            turned[stage, c, j] = ref[j // NY, j % NY, c].reshape(CHUNK, FEAT).T

    def encode(ref, c, result, stage, with_bias):
        total = None
        for m in range(NX):
            for at in range(NY):
                part = jnp.dot(ref[m, at, c].reshape(CHUNK, FEAT), dic[m * NY + at], preferred_element_type=F32)
                total = part if total is None else total + part
        pre[c, stage] = total
        mine = pl.ds(pl.multiple_of(core * 64, 64), 64)
        theirs = pl.ds(pl.multiple_of((1 - core) * 64, 64), 64)
        half_out[c, stage] = pre[c, stage, theirs, :].astype(BF16)
        copy = send(half_out.at[c, stage], half_in.at[c, stage], core_peer)
        turn(ref, c, stage, (0, 1))
        yield
        copy.wait_recv()
        half = (pre[c, stage, mine, :] + half_in[c, stage].astype(F32)).astype(BF16)
        pair_out[c, stage] = half
        copy = send(pair_out.at[c, stage], pair_in.at[c, stage], pair_peer)
        turn(ref, c, stage, range(2, NX * NY))
        store(turned.at[stage, c], turned_hbm.at[stage, c])
        yield
        copy.wait_recv()
        total = pair_out[c, stage].astype(F32) + pair_in[c, stage].astype(F32)
        if with_bias:
            total = total + bias[...]
        places = pl.ds(core * 4, 4)
        mask = act[places, c].reshape(64, LAT).astype(F32)
        result[c, places] = (mask * total).astype(BF16).reshape(4, ROWS, LAT)
        copy = send(result.at[c, places], result.at[c, places], core_peer)
        yield
        copy.wait_recv()

    def project(c):
        rows = attn[:, c].reshape(CHUNK, 256)
        for k in y_order + (0,):
            cols = pl.ds(pl.multiple_of(y_at[k] * FEAT, FEAT), FEAT)
            part = jnp.dot(rows, proj[:, cols], preferred_element_type=F32).reshape(NZ, ROWS, FEAT)
            if k == 0:
                proj_acc[c] = part
            else:
                proj_out[c, k] = part.astype(BF16)

    def chain(c):
        group = along_y(lambda k: proj_out.at[c, k], lambda k: proj_in.at[c, k], proj_in.at[c, pl.ds(1, 3)])
        yield
        group.wait_recv()
        summed = proj_acc[c]
        for k in range(1, 4):
            summed = summed + proj_in[c, k].astype(F32)
        proj_acc[c] = summed
        fold_out[c] = summed.astype(BF16)
        group = along_z(lambda k: fold_out.at[c, z_at[k]], lambda k: fold_in.at[c, k], fold_in.at[c, pl.ds(1, 7)])
        yield
        if c == 0:
            res_group.wait_recv()
        group.wait_recv()
        own = proj_acc[c, z]
        for k in range(1, 8):
            own = own + fold_in[c, k].astype(F32)
        upper = res_in[(y - 2 * c + 4) % 4]
        lower = res_in[(y - 2 * c + 3) % 4]
        fields[xh, y, c, z] = (own + jnp.concatenate([upper, lower], axis=0)).astype(BF16)
        yield from gather(fields, c)
        if c == 0:
            for copy in loads[3:]:
                copy.wait()
        yield from encode(fields, c, feats, 0, True)
        store(feats.at[c], feats_hbm.at[c])

        code = feats[c].reshape(CHUNK, LAT)

        def decode(j, cols):
            return nt_dot(code, dic[j, cols, :]).reshape(NZ, ROWS, HALF)

        for at in range(NY):
            xa_out[c, at] = decode((1 - xh) * NY + at, low).astype(BF16)
        xa_copy = send(xa_out.at[c], xa_in.at[c], x_peer)
        for k in y_order:
            for m in range(NX):
                yb_out[c, k, m] = decode(m * NY + y_at[k], high).astype(BF16)
        yb_group = along_y(lambda k: yb_out.at[c, k], lambda k: yb_in.at[c, k], yb_in.at[c, pl.ds(1, 3)])
        for at in range(NY):
            xa_own[c, at] = decode(xh * NY + at, low)
        for m in range(NX):
            yb_own[c, m] = decode(m * NY + y, high)
        yield
        xa_copy.wait_recv()
        for k in y_order + (0,):
            at = y_at[k]
            part = xa_own[c, at] + xa_in[c, at].astype(F32)
            if k == 0:
                z_own[c, :, :, :HALF] = part
            else:
                ya_out[c, k] = part.astype(BF16)
        ya_group = along_y(lambda k: ya_out.at[c, k], lambda k: ya_in.at[c, k], ya_in.at[c, pl.ds(1, 3)])
        yield
        yb_group.wait_recv()

        def over_y(m):
            part = yb_own[c, m]
            for k in range(1, 4):
                part = part + yb_in[c, k, m].astype(F32)
            return part

        xb_out[c] = over_y(1 - xh).astype(BF16)
        xb_copy = send(xb_out.at[c], xb_in.at[c], x_peer)
        z_own[c, :, :, HALF:] = over_y(xh)
        yield
        ya_group.wait_recv()
        part = z_own[c, :, :, :HALF]
        for k in range(1, 4):
            part = part + ya_in[c, k].astype(F32)
        z_own[c, :, :, :HALF] = part
        z_out[c, :, :, :HALF] = part.astype(BF16)
        xb_copy.wait_recv()
        part = z_own[c, :, :, HALF:] + xb_in[c].astype(F32)
        z_own[c, :, :, HALF:] = part
        z_out[c, :, :, HALF:] = part.astype(BF16)
        group = along_z(lambda k: z_out.at[c, z_at[k]], lambda k: z_in.at[c, k], z_in.at[c, pl.ds(1, 7)])
        yield
        group.wait_recv()
        recon = z_own[c, z]
        for k in range(1, 8):
            recon = recon + z_in[c, k].astype(F32)
        errors[xh, y, c, z] = (recon - fields[xh, y, c, z].astype(F32)).astype(BF16)
        yield from gather(errors, c)
        yield from encode(errors, c, gpre, 1, False)
        store(gpre.at[c], gpre_hbm.at[c])

    for copy in loads[:2]:
        copy.wait()
    project(0)
    loads[2].wait()
    for k in range(4):
        cols = pl.ds(pl.multiple_of(y_at[k] * FEAT, FEAT), FEAT)
        if k == 0:
            res_in[0] = resid[:, cols].astype(F32)
        else:
            res_out[k] = resid[:, cols].astype(F32)
    pl.semaphore_wait(barrier, len(partners))
    first, second = chain(0), chain(1)
    next(first)
    res_group = along_y(lambda k: res_out.at[k], lambda k: res_in.at[k], res_in.at[pl.ds(1, 3)])
    project(1)
    for turn_at, turn_of in enumerate(ORDER):
        if turn_at == len(ORDER) - 4:
            for group in groups[:-12]:
                group.wait_send()
        next((first, second)[int(turn_of)], None)
    for group in groups:
        group.wait_send()
    for copy in stores:
        copy.wait()


def gradient_kernel(turned, feats, gpre, grad_hbm, bias_grad, grad, out_sem):
    slope = gpre[...].reshape(2 * CHUNK, LAT)
    right = jnp.concatenate([slope, feats[...].reshape(2 * CHUNK, LAT)], axis=0)
    stores = []
    for j in range(NX * NY):
        left = jnp.concatenate([turned[s, c, j] for s in range(2) for c in range(2)], axis=1)
        grad[j] = jnp.dot(left, right, preferred_element_type=F32).astype(BF16)
        copy = pltpu.make_async_copy(grad.at[j], grad_hbm.at[j], out_sem.at[j])
        copy.start()
        stores.append(copy)
    bias_grad[...] = jnp.sum(slope.astype(F32), axis=0, keepdims=True)
    for copy in stores:
        copy.wait()


def body(attention, out_proj, residual, dictionary, enc_bias, active):
    hbm = pl.BlockSpec(memory_space=pl.ANY)
    vmem = pl.BlockSpec(memory_space=pltpu.VMEM)
    piece = (NX, NY, 2, NZ, ROWS, FEAT)
    code = (2, NZ, ROWS, LAT)
    half = (NZ, ROWS, HALF)
    flipped = (2, 2, NX * NY, FEAT, CHUNK)
    shapes = [flipped, code, code]
    turned, feats, gpre = pl.pallas_call(
        step_kernel,
        out_shape=[pltpu.VMEM(s, BF16) for s in shapes],
        in_specs=[pl.BlockSpec(memory_space=pltpu.HBM)] * 6,
        out_specs=[hbm] * 3,
        scratch_shapes=[
            pltpu.VMEM(flipped, BF16),
            pltpu.VMEM((NZ, 2, ROWS, 256), BF16),
            pltpu.VMEM((256, NY * FEAT), BF16),
            pltpu.VMEM((8, NY * FEAT), BF16),
            pltpu.VMEM((NX * NY, FEAT, LAT), BF16),
            pltpu.VMEM((1, LAT), F32),
            pltpu.VMEM((NZ, 2, ROWS, LAT), jnp.int32),
            pltpu.VMEM(piece, BF16),
            pltpu.VMEM(piece, BF16),
            pltpu.VMEM(code, BF16),
            pltpu.VMEM(code, BF16),
            pltpu.VMEM((4, 8, FEAT), F32),
            pltpu.VMEM((4, 8, FEAT), F32),
            pltpu.VMEM((2, NZ, ROWS, FEAT), F32),
            pltpu.VMEM((2, 4, NZ, ROWS, FEAT), BF16),
            pltpu.VMEM((2, 4, NZ, ROWS, FEAT), BF16),
            pltpu.VMEM((2, NZ, ROWS, FEAT), BF16),
            pltpu.VMEM((2, 8, ROWS, FEAT), BF16),
            pltpu.VMEM((2, 2, CHUNK, LAT), F32),
            pltpu.VMEM((2, 2, 64, LAT), BF16),
            pltpu.VMEM((2, 2, 64, LAT), BF16),
            pltpu.VMEM((2, 2, 64, LAT), BF16),
            pltpu.VMEM((2, 2, 64, LAT), BF16),
            pltpu.VMEM((2, NY) + half, BF16),
            pltpu.VMEM((2, NY) + half, BF16),
            pltpu.VMEM((2, NY) + half, F32),
            pltpu.VMEM((2, 4) + half, BF16),
            pltpu.VMEM((2, 4) + half, BF16),
            pltpu.VMEM((2, 4, NX) + half, BF16),
            pltpu.VMEM((2, 4, NX) + half, BF16),
            pltpu.VMEM((2, NX) + half, F32),
            pltpu.VMEM((2,) + half, BF16),
            pltpu.VMEM((2,) + half, BF16),
            pltpu.VMEM((2, NZ, ROWS, FEAT), F32),
            pltpu.VMEM((2, NZ, ROWS, FEAT), BF16),
            pltpu.VMEM((2, 8, ROWS, FEAT), BF16),
            pltpu.SemaphoreType.DMA((14,)),
            pltpu.SemaphoreType.DMA((SENDS,)),
            pltpu.SemaphoreType.DMA((SENDS,)),
        ],
        compiler_params=pltpu.CompilerParams(
            collective_id=0, has_side_effects=True, vmem_limit_bytes=50 << 20
        ),
        name="crosscoder_step",
    )(
        attention.reshape(NZ, 2, ROWS, 256),
        out_proj,
        residual,
        dictionary.reshape(NX * NY, FEAT, LAT),
        enc_bias.reshape(1, LAT),
        active.reshape(NZ, 2, ROWS, LAT),
    )
    grad, bias_grad = pl.pallas_call(
        gradient_kernel,
        out_shape=[
            jax.ShapeDtypeStruct((NX * NY, FEAT, LAT), BF16),
            jax.ShapeDtypeStruct((1, LAT), F32),
        ],
        in_specs=[vmem] * 3,
        out_specs=[hbm, vmem],
        scratch_shapes=[
            pltpu.VMEM((NX * NY, FEAT, LAT), BF16),
            pltpu.SemaphoreType.DMA((NX * NY,)),
        ],
        compiler_params=pltpu.CompilerParams(vmem_limit_bytes=24 << 20),
        name="dictionary_gradient",
    )(turned, feats, gpre)
    return grad.reshape(dictionary.shape), bias_grad.reshape(LAT)


def solution(mesh):
    in_specs = (
        P(None, "wide"),
        P("wide", "narrow"),
        P("wide", "narrow"),
        P(None, "narrow", "wide"),
        P("wide"),
        P(None, "wide"),
    )
    out_specs = (P(None, "narrow", "wide"), P("wide"))
    return jax.shard_map(body, mesh=mesh, in_specs=in_specs, out_specs=out_specs, check_vma=False)
```

```python
import jax
import jax.numpy as jnp
from jax import lax
from jax.experimental import pallas as pl
from jax.experimental.pallas import tpu as pltpu
from jax.sharding import PartitionSpec as P

MESH = pl.DeviceIdType.MESH
F32 = jnp.float32
BF16 = jnp.bfloat16
NX, NZ, NY = 2, 4, 4
NC = 4
ROWS = 16
CHUNK = NZ * ROWS
FEAT = 512
LAT = 512
SENDS = 93
HALF = 256
ORDER = ("10120312031002311020122031013321200321032", "310312233102310023110213221330123230232013")


def nt_dot(left, right):
    return lax.dot_general(left, right, (((1,), (1,)), ((), ())), preferred_element_type=F32)


def tn_dot(left, right):
    return lax.dot_general(left, right, (((0,), (0,)), ((), ())), preferred_element_type=F32)


def step_kernel(
    attn_hbm, proj_hbm, resid_hbm, dict_hbm, bias_hbm, act_hbm,
    turned_hbm, feats_hbm, gpre_hbm,
    turned, attn, proj, resid, dic, bias, act, fields, errors, feats, gpre,
    res_out, res_in,
    proj_acc, proj_out, proj_in, fold_out, fold_in,
    pre, half_out, half_in, pair_out, pair_in,
    xa_out, xa_in, xa_own, ya_out, ya_in,
    yb_out, yb_in, yb_own, xb_out, xb_in,
    z_own, z_out, z_in,
    local_sem, send_sem, recv_sem,
):
    wide = lax.axis_index("wide")
    narrow = lax.axis_index("narrow")
    xh, z, y = wide // 32, (wide // 4) % 8, wide % 4
    zh, zl = z // 2, z % 2
    xl, core = narrow // 2, narrow % 2

    def dev(xh_=xh, z_=z, y_=y, xl_=xl, core_=core):
        return ((xh_ * 8 + z_) * 4 + y_, xl_ * 2 + core_)

    x_peer = dev(xh_=1 - xh)
    pair_peer = dev(xl_=1 - xl)
    core_peer = dev(core_=1 - core)
    y_at = [(y + k) % 4 for k in range(4)]
    z_at = [(z + k) % 8 for k in range(8)]
    y_peer = [dev(y_=at) for at in y_at]
    z_peer = [dev(z_=at) for at in z_at]
    across = [dev(z_=z + 1 - 2 * zl, y_=at) for at in y_at]

    barrier = pltpu.get_barrier_semaphore()
    partners = [x_peer, pair_peer, core_peer] + y_peer[1:] + z_peer[1:] + across[1:]
    for peer in partners:
        pl.semaphore_signal(barrier, inc=1, device_id=peer, device_id_type=MESH)

    loads = []
    for src, dst in (
        (attn_hbm, attn), (proj_hbm, proj), (resid_hbm, resid),
        (bias_hbm, bias), (act_hbm, act), (dict_hbm, dic),
    ):
        copy = pltpu.make_async_copy(src, dst, local_sem.at[len(loads)])
        copy.start()
        loads.append(copy)

    groups = []
    stores = []

    class Group:
        def __init__(self, size, copies):
            slot = len(groups)
            self.size, self.sems, self.sent = size, (send_sem.at[slot], recv_sem.at[slot]), False
            for src, dst, peer in copies:
                pltpu.make_async_remote_copy(
                    src_ref=src, dst_ref=dst, send_sem=self.sems[0], recv_sem=self.sems[1],
                    device_id=peer, device_id_type=MESH,
                ).start()
            groups.append(self)

        def wait_recv(self):
            pltpu.make_async_copy(self.size, self.size, self.sems[1]).wait()

        def wait_send(self):
            if not self.sent:
                pltpu.make_async_copy(self.size, self.size, self.sems[0]).wait()
            self.sent = True

    def send(src, dst, peer):
        return Group(dst, [(src, dst, peer)])

    def along_y(src, dst, size):
        return Group(size, [(src(k), dst(k), y_peer[k]) for k in y_order])

    def along_z(src, dst, size):
        return Group(size, [(src(k), dst(k), z_peer[k]) for k in z_order])

    def store(src, dst):
        copy = pltpu.make_async_copy(src, dst, local_sem.at[len(loads) + len(stores)])
        copy.start()
        stores.append(copy)

    halves = (pl.ds(0, HALF), pl.ds(HALF, HALF))
    z_order = (4, 3, 5, 2, 6, 1, 7)
    y_order = (2, 1, 3)

    def gather(ref, c):
        own = ref.at[xh, y, zl, c, zh]
        group = along_z(lambda k: own, lambda k: own, fold_in.at[c, pl.ds(1, 7)])
        yield
        group.wait_recv()
        own_low, own_high = ref.at[xh, y, 0, c], ref.at[xh, y, 1, c]
        over_y = along_y(lambda k: own_low, lambda k: own_low, ref.at[xh, pl.ds(0, 3), 0, c])
        over_x = send(own_high, own_high, x_peer)
        yield
        over_y.wait_recv()
        all_low = ref.at[xh, :, 0, c]
        last_x = send(all_low, all_low, x_peer)
        yield
        over_x.wait_recv()
        both_high = ref.at[:, y, 1, c]
        last_y = along_y(lambda k: both_high, lambda k: both_high, ref.at[:, pl.ds(0, 3), 1, c])
        yield
        last_x.wait_recv()
        last_y.wait_recv()

    gathered = {}
    seen = []

    def once(name):
        seen.append(name)
        return seen.count(name) == 1

    def turn(ref, pair, stage, blocks):
        for j in blocks:
            for h in range(2):
                rows = ref[j // NY, j % NY, h, pl.ds(2 * pair, 2)].reshape(2 * CHUNK, HALF)
                turned[stage, pair, j, halves[h], :] = rows.T

    def encode(ref, c, result, stage, with_bias):
        gathered[stage, c // 2] = gathered.get((stage, c // 2), 0) + 1
        both = gathered[stage, c // 2] == 2
        total = None
        for m in range(NX):
            for at in range(NY):
                for h in range(2):
                    rows = ref[m, at, h, c].reshape(CHUNK, HALF)
                    part = jnp.dot(rows, dic[m * NY + at, halves[h], :], preferred_element_type=F32)
                    total = part if total is None else total + part
        pre[c, stage] = total
        mine = pl.ds(pl.multiple_of(core * 32, 32), 32)
        theirs = pl.ds(pl.multiple_of((1 - core) * 32, 32), 32)
        half_out[c, stage] = pre[c, stage, theirs, :].astype(BF16)
        copy = send(half_out.at[c, stage], half_in.at[c, stage], core_peer)
        if both:
            turn(ref, c // 2, stage, (0, 1))
        yield
        copy.wait_recv()
        half = (pre[c, stage, mine, :] + half_in[c, stage].astype(F32)).astype(BF16)
        pair_out[c, stage] = half
        copy = send(pair_out.at[c, stage], pair_in.at[c, stage], pair_peer)
        if both:
            turn(ref, c // 2, stage, range(2, NX * NY))
            store(turned.at[stage, c // 2], turned_hbm.at[stage, c // 2])
        yield
        copy.wait_recv()
        total = pair_out[c, stage].astype(F32) + pair_in[c, stage].astype(F32)
        if with_bias:
            total = total + bias[...]
        places = pl.ds(core * 2, 2)
        mask = act[places, c].reshape(32, LAT).astype(F32)
        result[c, places] = (mask * total).astype(BF16).reshape(2, ROWS, LAT)
        copy = send(result.at[c, places], result.at[c, places], core_peer)
        yield
        copy.wait_recv()

    def project(c):
        rows = attn[:, c].reshape(CHUNK, 256)
        for k in y_order + (0,):
            cols = pl.ds(pl.multiple_of(y_at[k] * FEAT, FEAT), FEAT)
            part = jnp.dot(rows, proj[:, cols], preferred_element_type=F32)
            for h in range(2):
                half = part[:, h * HALF:(h + 1) * HALF].reshape(NZ, ROWS, HALF)
                if k == 0:
                    proj_acc[c, h] = half
                else:
                    proj_out[c, k, h] = half.astype(BF16)

    def chain(c):
        group = along_y(lambda k: proj_out.at[c, k], lambda k: proj_in.at[c, k], proj_in.at[c, pl.ds(1, 3)])
        yield
        group.wait_recv()
        summed = proj_acc[c]
        for k in range(1, 4):
            summed = summed + proj_in[c, k].astype(F32)
        proj_acc[c] = summed
        fold_out[c] = summed.astype(BF16)
        group = along_z(lambda k: fold_out.at[c, z_at[k] % 2, z_at[k] // 2], lambda k: fold_in.at[c, k], fold_in.at[c, pl.ds(1, 7)])
        yield
        if once("residual"):
            res_group.wait_recv()
        group.wait_recv()
        own = proj_acc[c, zl, zh]
        for k in range(1, 8):
            own = own + fold_in[c, k].astype(F32)
        from_half = 4 * ((zl + c // 2) % 2)
        upper = res_in[from_half + (y - 2 * (c % 2) + 4) % 4]
        lower = res_in[from_half + (y - 2 * (c % 2) + 3) % 4]
        fields[xh, y, zl, c, zh] = (own + jnp.concatenate([upper, lower], axis=0)).astype(BF16)
        yield from gather(fields, c)
        if once("loads"):
            for copy in loads[3:]:
                copy.wait()
        yield from encode(fields, c, feats, 0, True)
        store(feats.at[c], feats_hbm.at[c])

        code = feats[c].reshape(CHUNK, LAT)

        def decode(j, h):
            return nt_dot(code, dic[j, halves[h], :]).reshape(NZ, ROWS, HALF)

        for at in range(NY):
            xa_out[c, at] = decode((1 - xh) * NY + at, 0).astype(BF16)
        xa_copy = send(xa_out.at[c], xa_in.at[c], x_peer)
        for k in y_order:
            for m in range(NX):
                yb_out[c, k, m] = decode(m * NY + y_at[k], 1).astype(BF16)
        yb_group = along_y(lambda k: yb_out.at[c, k], lambda k: yb_in.at[c, k], yb_in.at[c, pl.ds(1, 3)])
        for at in range(NY):
            xa_own[c, at] = decode(xh * NY + at, 0)
        for m in range(NX):
            yb_own[c, m] = decode(m * NY + y, 1)
        yield
        xa_copy.wait_recv()
        for k in y_order + (0,):
            at = y_at[k]
            part = xa_own[c, at] + xa_in[c, at].astype(F32)
            if k == 0:
                z_own[c, 0] = part
            else:
                ya_out[c, k] = part.astype(BF16)
        ya_group = along_y(lambda k: ya_out.at[c, k], lambda k: ya_in.at[c, k], ya_in.at[c, pl.ds(1, 3)])
        yield
        yb_group.wait_recv()

        def over_y(m):
            part = yb_own[c, m]
            for k in range(1, 4):
                part = part + yb_in[c, k, m].astype(F32)
            return part

        xb_out[c] = over_y(1 - xh).astype(BF16)
        xb_copy = send(xb_out.at[c], xb_in.at[c], x_peer)
        z_own[c, 1] = over_y(xh)
        yield
        ya_group.wait_recv()
        part = z_own[c, 0]
        for k in range(1, 4):
            part = part + ya_in[c, k].astype(F32)
        z_own[c, 0] = part
        z_out[c, 0] = part.astype(BF16)
        xb_copy.wait_recv()
        part = z_own[c, 1] + xb_in[c].astype(F32)
        z_own[c, 1] = part
        z_out[c, 1] = part.astype(BF16)
        group = along_z(lambda k: z_out.at[c, z_at[k] % 2, z_at[k] // 2], lambda k: z_in.at[c, k], z_in.at[c, pl.ds(1, 7)])
        yield
        group.wait_recv()
        recon = z_own[c, zl, zh]
        for k in range(1, 8):
            recon = recon + z_in[c, k].astype(F32)
        errors[xh, y, zl, c, zh] = (recon - fields[xh, y, zl, c, zh].astype(F32)).astype(BF16)
        yield from gather(errors, c)
        yield from encode(errors, c, gpre, 1, False)
        store(gpre.at[c], gpre_hbm.at[c])

    for copy in loads[:2]:
        copy.wait()
    project(0)
    loads[2].wait()
    for d in range(2):
        for k in range(4):
            start = y_at[k] * FEAT + ((zl + d) % 2) * HALF
            rows = resid[:, pl.ds(pl.multiple_of(start, HALF), HALF)].astype(F32)
            if d == 0 and k == 0:
                res_in[0] = rows
            else:
                res_out[4 * d + k] = rows
    pl.semaphore_wait(barrier, len(partners))
    chains = [chain(c) for c in range(NC)]
    next(chains[0])
    res_copies = [(res_out.at[k], res_in.at[k], y_peer[k]) for k in y_order]
    res_copies += [(res_out.at[4 + k], res_in.at[4 + k], across[k]) for k in (2, 1, 3, 0)]
    res_group = Group(res_in.at[pl.ds(1, 7)], res_copies)
    for c in range(1, NC):
        project(c)
    for turn_at, turn_of in enumerate(ORDER[0] + ORDER[1]):
        if turn_at == 3 * 21 + 20 - 6:
            for group in groups[:-20]:
                group.wait_send()
        next(chains[int(turn_of)], None)
    for group in groups:
        group.wait_send()
    for copy in stores:
        copy.wait()


def gradient_kernel(turned, feats, gpre, grad_hbm, bias_grad, grad, out_sem):
    slope = gpre[...].reshape(NC * CHUNK, LAT)
    right = jnp.concatenate([slope, feats[...].reshape(NC * CHUNK, LAT)], axis=0)
    stores = []
    for j in range(NX * NY):
        left = jnp.concatenate([turned[s, c, j] for s in range(2) for c in range(2)], axis=1)
        grad[j] = jnp.dot(left, right, preferred_element_type=F32).astype(BF16)
        copy = pltpu.make_async_copy(grad.at[j], grad_hbm.at[j], out_sem.at[j])
        copy.start()
        stores.append(copy)
    bias_grad[...] = jnp.sum(slope.astype(F32), axis=0, keepdims=True)
    for copy in stores:
        copy.wait()


def body(attention, out_proj, residual, dictionary, enc_bias, active):
    hbm = pl.BlockSpec(memory_space=pl.ANY)
    vmem = pl.BlockSpec(memory_space=pltpu.VMEM)
    half = (NZ, ROWS, HALF)
    piece = (NX, NY, 2, NC) + half
    code = (NC, NZ, ROWS, LAT)
    flipped = (2, 2, NX * NY, FEAT, 2 * CHUNK)
    narrow_half = (NC, 2, 32, LAT)
    shapes = [flipped, code, code]
    turned, feats, gpre = pl.pallas_call(
        step_kernel,
        out_shape=[pltpu.VMEM(s, BF16) for s in shapes],
        in_specs=[pl.BlockSpec(memory_space=pltpu.HBM)] * 6,
        out_specs=[hbm] * 3,
        scratch_shapes=[
            pltpu.VMEM(flipped, BF16),
            pltpu.VMEM((NZ, NC, ROWS, 256), BF16),
            pltpu.VMEM((256, NY * FEAT), BF16),
            pltpu.VMEM((8, NY * FEAT), BF16),
            pltpu.VMEM((NX * NY, FEAT, LAT), BF16),
            pltpu.VMEM((1, LAT), F32),
            pltpu.VMEM((NZ, NC, ROWS, LAT), jnp.int32),
            pltpu.VMEM(piece, BF16),
            pltpu.VMEM(piece, BF16),
            pltpu.VMEM(code, BF16),
            pltpu.VMEM(code, BF16),
            pltpu.VMEM((8, 8, HALF), F32),
            pltpu.VMEM((8, 8, HALF), F32),
            pltpu.VMEM((NC, 2) + half, F32),
            pltpu.VMEM((NC, 4, 2) + half, BF16),
            pltpu.VMEM((NC, 4, 2) + half, BF16),
            pltpu.VMEM((NC, 2) + half, BF16),
            pltpu.VMEM((NC, 8, ROWS, HALF), BF16),
            pltpu.VMEM((NC, 2, CHUNK, LAT), F32),
            pltpu.VMEM(narrow_half, BF16),
            pltpu.VMEM(narrow_half, BF16),
            pltpu.VMEM(narrow_half, BF16),
            pltpu.VMEM(narrow_half, BF16),
            pltpu.VMEM((NC, NY) + half, BF16),
            pltpu.VMEM((NC, NY) + half, BF16),
            pltpu.VMEM((NC, NY) + half, F32),
            pltpu.VMEM((NC, 4) + half, BF16),
            pltpu.VMEM((NC, 4) + half, BF16),
            pltpu.VMEM((NC, 4, NX) + half, BF16),
            pltpu.VMEM((NC, 4, NX) + half, BF16),
            pltpu.VMEM((NC, NX) + half, F32),
            pltpu.VMEM((NC,) + half, BF16),
            pltpu.VMEM((NC,) + half, BF16),
            pltpu.VMEM((NC, 2) + half, F32),
            pltpu.VMEM((NC, 2) + half, BF16),
            pltpu.VMEM((NC, 8, ROWS, HALF), BF16),
            pltpu.SemaphoreType.DMA((18,)),
            pltpu.SemaphoreType.DMA((SENDS,)),
            pltpu.SemaphoreType.DMA((SENDS,)),
        ],
        compiler_params=pltpu.CompilerParams(
            collective_id=0, has_side_effects=True, vmem_limit_bytes=50 << 20
        ),
        name="crosscoder_step",
    )(
        attention.reshape(NZ, NC, ROWS, 256),
        out_proj,
        residual,
        dictionary.reshape(NX * NY, FEAT, LAT),
        enc_bias.reshape(1, LAT),
        active.reshape(NZ, NC, ROWS, LAT),
    )
    grad, bias_grad = pl.pallas_call(
        gradient_kernel,
        out_shape=[
            jax.ShapeDtypeStruct((NX * NY, FEAT, LAT), BF16),
            jax.ShapeDtypeStruct((1, LAT), F32),
        ],
        in_specs=[vmem] * 3,
        out_specs=[hbm, vmem],
        scratch_shapes=[
            pltpu.VMEM((NX * NY, FEAT, LAT), BF16),
            pltpu.SemaphoreType.DMA((NX * NY,)),
        ],
        compiler_params=pltpu.CompilerParams(vmem_limit_bytes=24 << 20),
        name="dictionary_gradient",
    )(turned, feats, gpre)
    return grad.reshape(dictionary.shape), bias_grad.reshape(LAT)


def solution(mesh):
    in_specs = (
        P(None, "wide"),
        P("wide", "narrow"),
        P("wide", "narrow"),
        P(None, "narrow", "wide"),
        P("wide"),
        P(None, "wide"),
    )
    out_specs = (P(None, "narrow", "wide"), P("wide"))
    return jax.shard_map(body, mesh=mesh, in_specs=in_specs, out_specs=out_specs, check_vma=False)
```

```python
import jax
import jax.numpy as jnp
from jax import lax
from jax.experimental import pallas as pl
from jax.experimental.pallas import tpu as pltpu
from jax.sharding import PartitionSpec as P

MESH = pl.DeviceIdType.MESH
F32 = jnp.float32
BF16 = jnp.bfloat16
NX, NZ, NY = 2, 4, 4
NC = 4
ROWS = 16
CHUNK = NZ * ROWS
FEAT = 512
LAT = 512
SENDS = 93
HALF = 256
ORDER = ("10321012031002311020122013023321001203231", "013223102331020312311022031133223032103123")


def nt_dot(left, right):
    return lax.dot_general(left, right, (((1,), (1,)), ((), ())), preferred_element_type=F32)


def tn_dot(left, right):
    return lax.dot_general(left, right, (((0,), (0,)), ((), ())), preferred_element_type=F32)


def step_kernel(
    attn_hbm, proj_hbm, resid_hbm, dict_hbm, bias_hbm, act_hbm,
    turned_hbm, feats_hbm, gpre_hbm,
    turned, attn, proj, resid, dic, bias, act, fields, errors, feats, gpre,
    res_out, res_in,
    proj_acc, proj_out, proj_in, fold_out, fold_in,
    pre, half_out, half_in, pair_out, pair_in,
    xa_out, xa_in, xa_own, ya_out, ya_in,
    yb_out, yb_in, yb_own, xb_out, xb_in,
    z_own, z_out, z_in,
    local_sem, send_sem, recv_sem,
):
    wide = lax.axis_index("wide")
    narrow = lax.axis_index("narrow")
    xh, z, y = wide // 32, (wide // 4) % 8, wide % 4
    zh, zl = z // 2, z % 2
    xl, core = narrow // 2, narrow % 2

    def dev(xh_=xh, z_=z, y_=y, xl_=xl, core_=core):
        return ((xh_ * 8 + z_) * 4 + y_, xl_ * 2 + core_)

    x_peer = dev(xh_=1 - xh)
    pair_peer = dev(xl_=1 - xl)
    core_peer = dev(core_=1 - core)
    y_at = [(y + k) % 4 for k in range(4)]
    z_at = [(z + k) % 8 for k in range(8)]
    y_peer = [dev(y_=at) for at in y_at]
    z_peer = [dev(z_=at) for at in z_at]
    across = [dev(z_=z + 1 - 2 * zl, y_=at) for at in y_at]

    barrier = pltpu.get_barrier_semaphore()
    partners = [x_peer, pair_peer, core_peer] + y_peer[1:] + z_peer[1:] + across[1:]
    for peer in partners:
        pl.semaphore_signal(barrier, inc=1, device_id=peer, device_id_type=MESH)

    loads = []
    for src, dst in (
        (attn_hbm, attn), (proj_hbm, proj), (resid_hbm, resid),
        (bias_hbm, bias), (act_hbm, act), (dict_hbm, dic),
    ):
        copy = pltpu.make_async_copy(src, dst, local_sem.at[len(loads)])
        copy.start()
        loads.append(copy)

    groups = []
    stores = []

    class Group:
        def __init__(self, size, copies):
            slot = len(groups)
            self.size, self.sems, self.sent = size, (send_sem.at[slot], recv_sem.at[slot]), False
            for src, dst, peer in copies:
                pltpu.make_async_remote_copy(
                    src_ref=src, dst_ref=dst, send_sem=self.sems[0], recv_sem=self.sems[1],
                    device_id=peer, device_id_type=MESH,
                ).start()
            groups.append(self)

        def wait_recv(self):
            pltpu.make_async_copy(self.size, self.size, self.sems[1]).wait()

        def wait_send(self):
            if not self.sent:
                pltpu.make_async_copy(self.size, self.size, self.sems[0]).wait()
            self.sent = True

    def send(src, dst, peer):
        return Group(dst, [(src, dst, peer)])

    def along_y(src, dst, size):
        return Group(size, [(src(k), dst(k), y_peer[k]) for k in y_order])

    def along_z(src, dst, size):
        return Group(size, [(src(k), dst(k), z_peer[k]) for k in z_order])

    def store(src, dst):
        copy = pltpu.make_async_copy(src, dst, local_sem.at[len(loads) + len(stores)])
        copy.start()
        stores.append(copy)

    halves = (pl.ds(0, HALF), pl.ds(HALF, HALF))
    z_order = (4, 3, 5, 2, 6, 1, 7)
    y_order = (2, 1, 3)

    def gather(ref, c):
        own = ref.at[xh, y, zl, c, zh]
        group = along_z(lambda k: own, lambda k: own, fold_in.at[c, pl.ds(1, 7)])
        yield
        group.wait_recv()
        own_low, own_high = ref.at[xh, y, 0, c], ref.at[xh, y, 1, c]
        over_y = along_y(lambda k: own_low, lambda k: own_low, ref.at[xh, pl.ds(0, 3), 0, c])
        over_x = send(own_high, own_high, x_peer)
        yield
        over_y.wait_recv()
        all_low = ref.at[xh, :, 0, c]
        last_x = send(all_low, all_low, x_peer)
        yield
        over_x.wait_recv()
        both_high = ref.at[:, y, 1, c]
        last_y = along_y(lambda k: both_high, lambda k: both_high, ref.at[:, pl.ds(0, 3), 1, c])
        yield
        last_x.wait_recv()
        last_y.wait_recv()

    gathered = {}
    seen = []

    def once(name):
        seen.append(name)
        return seen.count(name) == 1

    def turn(ref, pair, stage, blocks):
        for j in blocks:
            for h in range(2):
                rows = ref[j // NY, j % NY, h, pl.ds(2 * pair, 2)].reshape(2 * CHUNK, HALF)
                turned[stage, pair, j, halves[h], :] = rows.T

    def encode(ref, c, result, stage, with_bias):
        gathered[stage, c // 2] = gathered.get((stage, c // 2), 0) + 1
        both = gathered[stage, c // 2] == 2
        total = None
        for m in range(NX):
            for at in range(NY):
                for h in range(2):
                    rows = ref[m, at, h, c].reshape(CHUNK, HALF)
                    part = jnp.dot(rows, dic[m * NY + at, halves[h], :], preferred_element_type=F32)
                    total = part if total is None else total + part
        pre[c, stage] = total
        mine = pl.ds(pl.multiple_of(core * 32, 32), 32)
        theirs = pl.ds(pl.multiple_of((1 - core) * 32, 32), 32)
        half_out[c, stage] = pre[c, stage, theirs, :].astype(BF16)
        copy = send(half_out.at[c, stage], half_in.at[c, stage], core_peer)
        if both:
            turn(ref, c // 2, stage, (0, 1))
        yield
        copy.wait_recv()
        half = (pre[c, stage, mine, :] + half_in[c, stage].astype(F32)).astype(BF16)
        pair_out[c, stage] = half
        copy = send(pair_out.at[c, stage], pair_in.at[c, stage], pair_peer)
        if both:
            turn(ref, c // 2, stage, range(2, NX * NY))
            store(turned.at[stage, c // 2], turned_hbm.at[stage, c // 2])
        yield
        copy.wait_recv()
        total = pair_out[c, stage].astype(F32) + pair_in[c, stage].astype(F32)
        if with_bias:
            total = total + bias[...]
        places = pl.ds(core * 2, 2)
        mask = act[places, c].reshape(32, LAT).astype(F32)
        result[c, places] = (mask * total).astype(BF16).reshape(2, ROWS, LAT)
        place = result.at[c, places]
        if stage:
            place = gpre_hbm.at[c, places]
            store(result.at[c, places], place)
        copy = send(result.at[c, places], place, core_peer)
        yield
        copy.wait_recv()

    def project(c):
        rows = attn[:, c].reshape(CHUNK, 256)
        for k in y_order + (0,):
            cols = pl.ds(pl.multiple_of(y_at[k] * FEAT, FEAT), FEAT)
            part = jnp.dot(rows, proj[:, cols], preferred_element_type=F32)
            for h in range(2):
                half = part[:, h * HALF:(h + 1) * HALF].reshape(NZ, ROWS, HALF)
                if k == 0:
                    proj_acc[c, h] = half
                else:
                    proj_out[c, k, h] = half.astype(BF16)

    def chain(c):
        group = along_y(lambda k: proj_out.at[c, k], lambda k: proj_in.at[c, k], proj_in.at[c, pl.ds(1, 3)])
        yield
        group.wait_recv()
        summed = proj_acc[c]
        for k in range(1, 4):
            summed = summed + proj_in[c, k].astype(F32)
        proj_acc[c] = summed
        fold_out[c] = summed.astype(BF16)
        group = along_z(lambda k: fold_out.at[c, z_at[k] % 2, z_at[k] // 2], lambda k: fold_in.at[c, k], fold_in.at[c, pl.ds(1, 7)])
        yield
        if once("residual"):
            res_group.wait_recv()
        group.wait_recv()
        own = proj_acc[c, zl, zh]
        for k in range(1, 8):
            own = own + fold_in[c, k].astype(F32)
        from_half = 4 * ((zl + c // 2) % 2)
        upper = res_in[from_half + (y - 2 * (c % 2) + 4) % 4]
        lower = res_in[from_half + (y - 2 * (c % 2) + 3) % 4]
        fields[xh, y, zl, c, zh] = (own + jnp.concatenate([upper, lower], axis=0)).astype(BF16)
        yield from gather(fields, c)
        if once("loads"):
            for copy in loads[3:]:
                copy.wait()
        yield from encode(fields, c, feats, 0, True)
        store(feats.at[c], feats_hbm.at[c])

        code = feats[c].reshape(CHUNK, LAT)

        def decode(j, h):
            return nt_dot(code, dic[j, halves[h], :]).reshape(NZ, ROWS, HALF)

        for at in range(NY):
            xa_out[c, at] = decode((1 - xh) * NY + at, 0).astype(BF16)
        xa_copy = send(xa_out.at[c], xa_in.at[c], x_peer)
        for k in y_order:
            for m in range(NX):
                yb_out[c, k, m] = decode(m * NY + y_at[k], 1).astype(BF16)
        yb_group = along_y(lambda k: yb_out.at[c, k], lambda k: yb_in.at[c, k], yb_in.at[c, pl.ds(1, 3)])
        for at in range(NY):
            xa_own[c, at] = decode(xh * NY + at, 0)
        for m in range(NX):
            yb_own[c, m] = decode(m * NY + y, 1)
        yield
        xa_copy.wait_recv()
        for k in y_order + (0,):
            at = y_at[k]
            part = xa_own[c, at] + xa_in[c, at].astype(F32)
            if k == 0:
                z_own[c, 0] = part
            else:
                ya_out[c, k] = part.astype(BF16)
        ya_group = along_y(lambda k: ya_out.at[c, k], lambda k: ya_in.at[c, k], ya_in.at[c, pl.ds(1, 3)])
        yield
        yb_group.wait_recv()

        def over_y(m):
            part = yb_own[c, m]
            for k in range(1, 4):
                part = part + yb_in[c, k, m].astype(F32)
            return part

        xb_out[c] = over_y(1 - xh).astype(BF16)
        xb_copy = send(xb_out.at[c], xb_in.at[c], x_peer)
        z_own[c, 1] = over_y(xh)
        yield
        ya_group.wait_recv()
        part = z_own[c, 0]
        for k in range(1, 4):
            part = part + ya_in[c, k].astype(F32)
        z_own[c, 0] = part
        z_out[c, 0] = part.astype(BF16)
        xb_copy.wait_recv()
        part = z_own[c, 1] + xb_in[c].astype(F32)
        z_own[c, 1] = part
        z_out[c, 1] = part.astype(BF16)
        group = along_z(lambda k: z_out.at[c, z_at[k] % 2, z_at[k] // 2], lambda k: z_in.at[c, k], z_in.at[c, pl.ds(1, 7)])
        yield
        group.wait_recv()
        recon = z_own[c, zl, zh]
        for k in range(1, 8):
            recon = recon + z_in[c, k].astype(F32)
        errors[xh, y, zl, c, zh] = (recon - fields[xh, y, zl, c, zh].astype(F32)).astype(BF16)
        yield from gather(errors, c)
        yield from encode(errors, c, gpre, 1, False)

    for copy in loads[:2]:
        copy.wait()
    project(0)
    loads[2].wait()
    for d in range(2):
        for k in range(4):
            start = y_at[k] * FEAT + ((zl + d) % 2) * HALF
            rows = resid[:, pl.ds(pl.multiple_of(start, HALF), HALF)].astype(F32)
            if d == 0 and k == 0:
                res_in[0] = rows
            else:
                res_out[4 * d + k] = rows
    pl.semaphore_wait(barrier, len(partners))
    chains = [chain(c) for c in range(NC)]
    next(chains[0])
    res_copies = [(res_out.at[k], res_in.at[k], y_peer[k]) for k in y_order]
    res_copies += [(res_out.at[4 + k], res_in.at[4 + k], across[k]) for k in (2, 1, 3, 0)]
    res_group = Group(res_in.at[pl.ds(1, 7)], res_copies)
    for c in range(1, NC):
        project(c)
    for turn_at, turn_of in enumerate(ORDER[0] + ORDER[1]):
        if turn_at == 3 * 21 + 20 - 6:
            for group in groups[:-20]:
                group.wait_send()
        next(chains[int(turn_of)], None)
    for group in groups:
        group.wait_send()
    for copy in stores:
        copy.wait()


def gradient_kernel(turned, feats, gpre, grad_hbm, bias_grad, grad, out_sem):
    slope = gpre[...].reshape(NC * CHUNK, LAT)
    right = jnp.concatenate([slope, feats[...].reshape(NC * CHUNK, LAT)], axis=0)
    stores = []
    for j in range(NX * NY):
        left = jnp.concatenate([turned[s, c, j] for s in range(2) for c in range(2)], axis=1)
        grad[j] = jnp.dot(left, right, preferred_element_type=F32).astype(BF16)
        copy = pltpu.make_async_copy(grad.at[j], grad_hbm.at[j], out_sem.at[j])
        copy.start()
        stores.append(copy)
    bias_grad[...] = jnp.sum(slope.astype(F32), axis=0, keepdims=True)
    for copy in stores:
        copy.wait()


def body(attention, out_proj, residual, dictionary, enc_bias, active):
    hbm = pl.BlockSpec(memory_space=pl.ANY)
    vmem = pl.BlockSpec(memory_space=pltpu.VMEM)
    half = (NZ, ROWS, HALF)
    piece = (NX, NY, 2, NC) + half
    code = (NC, NZ, ROWS, LAT)
    flipped = (2, 2, NX * NY, FEAT, 2 * CHUNK)
    narrow_half = (NC, 2, 32, LAT)
    shapes = [flipped, code, code]
    turned, feats, gpre = pl.pallas_call(
        step_kernel,
        out_shape=[pltpu.VMEM(s, BF16) for s in shapes],
        in_specs=[pl.BlockSpec(memory_space=pltpu.HBM)] * 6,
        out_specs=[hbm] * 3,
        scratch_shapes=[
            pltpu.VMEM(flipped, BF16),
            pltpu.VMEM((NZ, NC, ROWS, 256), BF16),
            pltpu.VMEM((256, NY * FEAT), BF16),
            pltpu.VMEM((8, NY * FEAT), BF16),
            pltpu.VMEM((NX * NY, FEAT, LAT), BF16),
            pltpu.VMEM((1, LAT), F32),
            pltpu.VMEM((NZ, NC, ROWS, LAT), jnp.int32),
            pltpu.VMEM(piece, BF16),
            pltpu.VMEM(piece, BF16),
            pltpu.VMEM(code, BF16),
            pltpu.VMEM(code, BF16),
            pltpu.VMEM((8, 8, HALF), F32),
            pltpu.VMEM((8, 8, HALF), F32),
            pltpu.VMEM((NC, 2) + half, F32),
            pltpu.VMEM((NC, 4, 2) + half, BF16),
            pltpu.VMEM((NC, 4, 2) + half, BF16),
            pltpu.VMEM((NC, 2) + half, BF16),
            pltpu.VMEM((NC, 8, ROWS, HALF), BF16),
            pltpu.VMEM((NC, 2, CHUNK, LAT), F32),
            pltpu.VMEM(narrow_half, BF16),
            pltpu.VMEM(narrow_half, BF16),
            pltpu.VMEM(narrow_half, BF16),
            pltpu.VMEM(narrow_half, BF16),
            pltpu.VMEM((NC, NY) + half, BF16),
            pltpu.VMEM((NC, NY) + half, BF16),
            pltpu.VMEM((NC, NY) + half, F32),
            pltpu.VMEM((NC, 4) + half, BF16),
            pltpu.VMEM((NC, 4) + half, BF16),
            pltpu.VMEM((NC, 4, NX) + half, BF16),
            pltpu.VMEM((NC, 4, NX) + half, BF16),
            pltpu.VMEM((NC, NX) + half, F32),
            pltpu.VMEM((NC,) + half, BF16),
            pltpu.VMEM((NC,) + half, BF16),
            pltpu.VMEM((NC, 2) + half, F32),
            pltpu.VMEM((NC, 2) + half, BF16),
            pltpu.VMEM((NC, 8, ROWS, HALF), BF16),
            pltpu.SemaphoreType.DMA((18,)),
            pltpu.SemaphoreType.DMA((SENDS,)),
            pltpu.SemaphoreType.DMA((SENDS,)),
        ],
        compiler_params=pltpu.CompilerParams(
            collective_id=0, has_side_effects=True, vmem_limit_bytes=50 << 20
        ),
        name="crosscoder_step",
    )(
        attention.reshape(NZ, NC, ROWS, 256),
        out_proj,
        residual,
        dictionary.reshape(NX * NY, FEAT, LAT),
        enc_bias.reshape(1, LAT),
        active.reshape(NZ, NC, ROWS, LAT),
    )
    grad, bias_grad = pl.pallas_call(
        gradient_kernel,
        out_shape=[
            jax.ShapeDtypeStruct((NX * NY, FEAT, LAT), BF16),
            jax.ShapeDtypeStruct((1, LAT), F32),
        ],
        in_specs=[vmem] * 3,
        out_specs=[hbm, vmem],
        scratch_shapes=[
            pltpu.VMEM((NX * NY, FEAT, LAT), BF16),
            pltpu.SemaphoreType.DMA((NX * NY,)),
        ],
        compiler_params=pltpu.CompilerParams(vmem_limit_bytes=24 << 20),
        name="dictionary_gradient",
    )(turned, feats, gpre)
    return grad.reshape(dictionary.shape), bias_grad.reshape(LAT)


def solution(mesh):
    in_specs = (
        P(None, "wide"),
        P("wide", "narrow"),
        P("wide", "narrow"),
        P(None, "narrow", "wide"),
        P("wide"),
        P(None, "wide"),
    )
    out_specs = (P(None, "narrow", "wide"), P("wide"))
    return jax.shard_map(body, mesh=mesh, in_specs=in_specs, out_specs=out_specs, check_vma=False)
```
